32 devices in a mesh: pipe: 4 (over z), expert: 4 (over x, core), tensor: 2 (over y).
Axes of the slice: x: 2, y: 2, z: 4, core: 2. Of those that a mesh axis runs over, the one named last changes fastest.
Arguments:
- acts: bfloat16 [4, 4, 256, 1792], P('pipe', 'expert'), may hold values from -6 to 6
- hidden_grad: bfloat16 [4, 2, 256, 1024], P('pipe', None, None, 'tensor'), may hold values from -0.5 to 0.5
- counts: int32 [4, 2, 2], P('pipe'), may hold values from 32 to 128, as said below
- momentum: bfloat16 [4, 4, 1792, 1024], P('pipe', 'expert', 'tensor'), may hold values from -6 to 6
- act_grad: bfloat16 [4, 256, 7168], P('pipe', 'expert', 'tensor'), may hold values from -6 to 6
Outputs:
- new_momentum: bfloat16 [4, 4, 1792, 1024], P('pipe', 'expert', 'tensor')
- gram_rows: float32 [4, 4, 256, 1024], P('pipe', 'expert', 'tensor')
- received: bfloat16 [4, 256, 7168], P('pipe', 'expert', 'tensor')
The draws below stay inside these ranges and needn't reach their ends.
Inputs may be any that keep to these rules, and one draw needn't show every extreme that they name: `counts`: in every section and expert, at least one micro-batch fills its block.
All inputs are finite; a program needn't handle non-finite values.
Results may differ from the reference program's by a relative error of at most 0.0065.
Values may be sent and summed in bfloat16 or wider, within the bound.
A program may use at most 64 MiB of HBM per device.

```python
import jax
import jax.numpy as jnp
from jax import lax

D = 3584
H = 1024
DM = 7168
PANEL = 512
BLOCK = 128
MICRO = 2
ROWS = 256
SECTIONS = 4
EXPERTS = 2
SLOTS = 4
TOK = 256
N_TENSOR = 2


def draw_counts(key, part):
    first_key, second_key = jax.random.split(key)
    shape_all = (SECTIONS, EXPERTS, MICRO)
    base_counts = jax.random.randint(first_key, shape_all, BLOCK // 4, BLOCK + 1)
    full_slot = jax.random.randint(second_key, (SECTIONS, EXPERTS, 1), 0, MICRO)
    slot_index = lax.broadcasted_iota(jnp.int32, shape_all, 2)
    return jnp.where(slot_index == full_slot, BLOCK, base_counts).astype(jnp.int32)


def block_scale(stream_key, dims, shards, low, high):
    def one(axis_at, blocks):
        steps = jax.random.uniform(jax.random.fold_in(jax.random.fold_in(stream_key, 6), axis_at), (blocks,), jnp.float32, low / len(shards), high / len(shards))
        return jnp.repeat(jnp.exp(steps), dims[axis_at] // blocks).reshape((-1,) + (1,) * (len(dims) - axis_at - 1))

    loudness = one(*shards[0])
    for cut in shards[1:]:
        loudness = loudness * one(*cut)
    return loudness


def centred(key, dims, width, most, pieces=(), held_as=jnp.bfloat16):
    gain = block_scale(key, dims, pieces, -0.22, 0.18) if pieces else 1.0
    array = jax.random.normal(key, dims, jnp.float32) * width * gain
    return jnp.minimum(jnp.maximum(array, -most), most).astype(held_as)


def setup_inputs(seed: int = 0) -> dict:
    seeds = jax.random.split(jax.random.key(seed), 6)
    return {
        "acts": centred(seeds[0], (SECTIONS, SLOTS, ROWS, D // 2), 1.0, 6.0, ((0, 4), (1, 4))),
        "hidden_grad": centred(seeds[1], (SECTIONS, EXPERTS, ROWS, H), 0.08, 0.5, ((0, 4), (3, 2))),
        "counts": draw_counts(jax.random.fold_in(seeds[5], 71), 0),
        "momentum": centred(seeds[3], (SECTIONS, SLOTS, D // 2, H), 1.0, 6.0, ((0, 4), (1, 4), (2, 2))),
        "act_grad": centred(seeds[4], (SECTIONS, TOK, DM), 1.0, 6.0, ((0, 4), (1, 4), (2, 2))),
    }


def contract(left, right):
    return lax.dot_general(left, right, (((0,), (0,)), ((), ())), preferred_element_type=jnp.float32)


def one_expert(inputs):
    features, gradients, counts_row, moment = inputs
    live_rows = (counts_row[:, None] > jnp.arange(BLOCK, dtype=jnp.int32)[None, :]).reshape(-1)
    masked = jnp.where(live_rows[:, None], gradients, jnp.zeros_like(gradients))
    grad_w = contract(features, masked).astype(jnp.bfloat16)
    new_full = (0.9 * moment.astype(jnp.float32) + grad_w.astype(jnp.float32)).astype(jnp.bfloat16)
    gram_full = contract(new_full[:, :PANEL], new_full) / D
    quarter = PANEL // (2 * N_TENSOR)
    gram_split = gram_full.reshape(N_TENSOR, 2, quarter, H).transpose(1, 0, 2, 3).reshape(2, PANEL // 2, H)
    return new_full, gram_split


def reference(acts, hidden_grad, counts, momentum, act_grad):
    total = SECTIONS * EXPERTS
    features = acts.reshape(SECTIONS, EXPERTS, 2, ROWS, D // 2).transpose(0, 1, 3, 2, 4).reshape(total, ROWS, D)
    moments = momentum.reshape(total, D, H)
    new_full, gram_split = lax.map(one_expert, (features, hidden_grad.reshape(total, ROWS, H), counts.reshape(total, MICRO), moments))
    new_momentum = new_full.reshape(SECTIONS, SLOTS, D // 2, H)
    gram_rows = gram_split.reshape(SECTIONS, SLOTS, PANEL // 2, H)
    received = jnp.concatenate([act_grad[1:], jnp.zeros_like(act_grad[:1])], axis=0)
    return (new_momentum, gram_rows, received)
```

```python
import functools

import jax
import jax.numpy as jnp
from jax import lax
from jax.experimental import pallas as pl
from jax.experimental.pallas import tpu as pltpu
from jax.sharding import PartitionSpec as P

D = 3584
PANEL = 512
DECAY = 0.9
MESH = pl.DeviceIdType.MESH


def contract(left, right):
    return lax.dot_general(
        left, right, (((0,), (0,)), ((), ())), preferred_element_type=jnp.float32
    )


def kernel(
    sections, ranks,
    acts, hidden, counts, momentum, act_grad,
    new_momentum, gram, received,
    x_buf, g_own, m_buf, n_buf, xt_buf, g_in, panel,
    send1, recv1, send2, recv2, gram_buf, zero_buf,
    load_sem, store_sem, shift_send, shift_recv,
    g_send, g_recv, f_send, f_recv, s1_send, s1_recv, s2_send, s2_recv,
):
    section = lax.axis_index("pipe")
    expert_rank = lax.axis_index("expert")
    rank = lax.axis_index("tensor")
    pair = expert_rank // 2
    half = expert_rank % 2
    partner = {"expert": expert_rank + 1 - 2 * half}
    row_count, features = x_buf.shape
    rows, hidden_units = n_buf.shape
    width = g_own.shape[1]
    part = width // 2
    q = send1.shape[1]
    first, last = section == 0, section == sections - 1

    if features == rows:
        x_src = acts.at[0, 0, :, pl.ds(pl.multiple_of(rank * rows, 128), rows)]
    else:
        x_src = acts.at[0, 0]
    load_x = pltpu.make_async_copy(x_src, x_buf, load_sem.at[0])
    load_g = pltpu.make_async_copy(hidden.at[0, pair], g_own, load_sem.at[1])
    load_m = pltpu.make_async_copy(momentum.at[0, 0], m_buf, load_sem.at[2])
    load_x.start()
    load_g.start()
    load_m.start()

    barrier = pltpu.get_barrier_semaphore()
    pl.semaphore_signal(barrier, inc=1, device_id=partner, device_id_type=MESH)
    for k in range(1, ranks):
        pl.semaphore_signal(
            barrier, inc=1, device_id={"tensor": (rank + k) % ranks}, device_id_type=MESH
        )

    @pl.when(jnp.logical_not(first))
    def _():
        pl.semaphore_signal(barrier, inc=1, device_id={"pipe": section - 1}, device_id_type=MESH)

    @pl.when(jnp.logical_not(last))
    def _():
        pl.semaphore_signal(barrier, inc=1, device_id={"pipe": section + 1}, device_id_type=MESH)

    ends = jnp.where(first, 1, 0) + jnp.where(last, 1, 0)
    pl.semaphore_wait(barrier, ranks + 2 - ends)

    def send_share(peer):
        return pltpu.make_async_remote_copy(
            src_ref=hidden.at[0, pair, :, pl.ds(pl.multiple_of(half * part, 128), part)],
            dst_ref=g_in.at[rank, half],
            send_sem=g_send.at[peer],
            recv_sem=g_recv.at[rank],
            device_id={"tensor": peer},
            device_id_type=MESH,
        )

    def arrived_share(peer):
        return pltpu.make_async_remote_copy(
            src_ref=g_in.at[peer, half],
            dst_ref=g_in.at[peer, half],
            send_sem=g_send.at[peer],
            recv_sem=g_recv.at[peer],
            device_id={"tensor": peer},
            device_id_type=MESH,
        )

    def forward(peer, which):
        return pltpu.make_async_remote_copy(
            src_ref=g_in.at[peer, which],
            dst_ref=g_in.at[peer, which],
            send_sem=f_send.at[peer],
            recv_sem=f_recv.at[peer],
            device_id=partner,
            device_id_type=MESH,
        )

    peers = [(rank + k) % ranks for k in range(1, ranks)]
    for peer in peers:
        send_share(peer).start()

    shift = pltpu.make_async_remote_copy(
        src_ref=act_grad,
        dst_ref=received,
        send_sem=shift_send,
        recv_sem=shift_recv,
        device_id={"pipe": section - 1},
        device_id_type=MESH,
    )

    @pl.when(jnp.logical_not(first))
    def _():
        shift.start()

    load_x.wait()
    row = lax.broadcasted_iota(jnp.int32, (row_count, 1), 0)
    micro = counts.shape[2]
    block = row_count // micro
    limit = jnp.zeros((row_count, 1), jnp.int32)
    for b in range(micro):
        inside = jnp.logical_and(row >= b * block, row < (b + 1) * block)
        limit = jnp.where(inside, counts[0, pair, b] + b * block, limit)
    live = jnp.where(row < limit, 1.0, 0.0).astype(jnp.float32)
    masked = (x_buf[...].astype(jnp.float32) * live).astype(jnp.bfloat16)
    xt_buf[...] = masked.T

    def update(start, size, gradients):
        cols = pl.ds(pl.multiple_of(start, 128), size)
        if features == rows:
            x_rows = xt_buf[...]
        else:
            x_rows = xt_buf[pl.ds(pl.multiple_of(rank * rows, 16), rows), :]
        grad = jnp.dot(x_rows, gradients, preferred_element_type=jnp.float32)
        grad = grad.astype(jnp.bfloat16).astype(jnp.float32)
        n_buf[:, cols] = (DECAY * m_buf[:, cols].astype(jnp.float32) + grad).astype(jnp.bfloat16)

    load_g.wait()
    load_m.wait()
    update(rank * width, width, g_own[...])

    @pl.when(last)
    def _():
        zero_buf[...] = jnp.zeros_like(zero_buf)
        pltpu.make_async_copy(zero_buf, received, store_sem.at[2]).start()

    for peer in peers:
        arrived_share(peer).wait_recv()
        forward(peer, half).start()
        update(peer * width + half * part, part, g_in[peer, half])
    for peer in peers:
        forward(peer, 1 - half).wait_recv()
        update(peer * width + (1 - half) * part, part, g_in[peer, 1 - half])
    store_n = pltpu.make_async_copy(n_buf, new_momentum, store_sem.at[0])
    store_n.start()

    def pair_rows(owner):
        return pltpu.make_async_remote_copy(
            src_ref=send1.at[owner],
            dst_ref=recv1.at[owner],
            send_sem=s1_send.at[owner],
            recv_sem=s1_recv.at[owner],
            device_id=partner,
            device_id_type=MESH,
        )

    def rank_rows(peer, slot):
        return pltpu.make_async_remote_copy(
            src_ref=send2.at[peer],
            dst_ref=recv2.at[slot],
            send_sem=s2_send.at[peer],
            recv_sem=s2_recv.at[slot],
            device_id={"tensor": peer},
            device_id_type=MESH,
        )

    def own_half(owner):
        return panel[owner, pl.ds(pl.multiple_of(half * q, q), q), :]

    for owner in peers + [rank]:
        start = pl.multiple_of(owner * 2 * q, 128)
        panel[owner] = contract(n_buf[:, pl.ds(start, 2 * q)], n_buf[...])
        other = panel[owner, pl.ds(pl.multiple_of((1 - half) * q, q), q), :]
        send1[owner] = other.astype(jnp.bfloat16)
        pair_rows(owner).start()
    for owner in peers:
        pair_rows(owner).wait_recv()
        send2[owner] = (own_half(owner) + recv1[owner].astype(jnp.float32)).astype(jnp.bfloat16)
        rank_rows(owner, rank).start()
    pair_rows(rank).wait_recv()
    total = own_half(rank) + recv1[rank].astype(jnp.float32)
    for peer in peers:
        rank_rows(peer, peer).wait_recv()
        total = total + recv2[peer].astype(jnp.float32)
    gram_buf[...] = total / D
    store_gram = pltpu.make_async_copy(gram_buf, gram, store_sem.at[1])
    store_gram.start()

    for peer in peers:
        send_share(peer).wait_send()
        forward(peer, half).wait_send()
        rank_rows(peer, rank).wait_send()
    for owner in peers + [rank]:
        pair_rows(owner).wait_send()

    @pl.when(jnp.logical_not(first))
    def _():
        shift.wait_send()

    @pl.when(jnp.logical_not(last))
    def _():
        shift.wait_recv()

    @pl.when(last)
    def _():
        pltpu.make_async_copy(zero_buf, received, store_sem.at[2]).wait()

    store_n.wait()
    store_gram.wait()


def on_device(acts, hidden_grad, counts, momentum, act_grad):
    sections, ranks = lax.axis_size("pipe"), lax.axis_size("tensor")
    row_count, features = acts.shape[2:]
    rows, units = momentum.shape[2:]
    width = hidden_grad.shape[3]
    q = PANEL // (2 * ranks)
    x_cols = rows if rows % 128 == 0 else features
    bf16, f32 = jnp.bfloat16, jnp.float32
    dma = pltpu.SemaphoreType.DMA
    hbm = pl.BlockSpec(memory_space=pl.ANY)
    new_momentum, gram, received = pl.pallas_call(
        functools.partial(kernel, sections, ranks),
        out_shape=(
            jax.ShapeDtypeStruct((rows, units), bf16),
            jax.ShapeDtypeStruct((q, units), f32),
            jax.ShapeDtypeStruct(act_grad.shape, bf16),
        ),
        in_specs=[hbm, hbm, pl.BlockSpec(memory_space=pltpu.SMEM), hbm, hbm],
        out_specs=(hbm, hbm, hbm),
        scratch_shapes=[
            pltpu.VMEM((row_count, x_cols), bf16),
            pltpu.VMEM((row_count, width), bf16),
            pltpu.VMEM((rows, units), bf16),
            pltpu.VMEM((rows, units), bf16),
            pltpu.VMEM((x_cols, row_count), bf16),
            pltpu.VMEM((ranks, 2, row_count, width // 2), bf16),
            pltpu.VMEM((ranks, 2 * q, units), f32),
            pltpu.VMEM((ranks, q, units), bf16),
            pltpu.VMEM((ranks, q, units), bf16),
            pltpu.VMEM((ranks, q, units), bf16),
            pltpu.VMEM((ranks, q, units), bf16),
            pltpu.VMEM((q, units), f32),
            pltpu.VMEM(act_grad.shape, bf16),
            dma((3,)), dma((3,)), dma, dma,
            dma((ranks,)), dma((ranks,)), dma((ranks,)), dma((ranks,)),
            dma((ranks,)), dma((ranks,)), dma((ranks,)), dma((ranks,)),
        ],
        compiler_params=pltpu.CompilerParams(
            collective_id=0, has_side_effects=True, vmem_limit_bytes=60 * 2**20
        ),
    )(acts, hidden_grad, counts, momentum, act_grad)
    return (new_momentum[None, None], gram[None, None], received)


def solution(mesh):
    return jax.shard_map(
        on_device,
        mesh=mesh,
        in_specs=(
            P("pipe", "expert", None, None),
            P("pipe", None, None, "tensor"),
            P("pipe", None, None),
            P("pipe", "expert", "tensor", None),
            P("pipe", "expert", "tensor"),
        ),
        out_specs=(
            P("pipe", "expert", "tensor", None),
            P("pipe", "expert", "tensor", None),
            P("pipe", "expert", "tensor"),
        ),
        check_vma=False,
    )
```

```python
import functools

import jax
import jax.numpy as jnp
from jax import lax
from jax.experimental import pallas as pl
from jax.experimental.pallas import tpu as pltpu
from jax.sharding import PartitionSpec as P

D = 3584
PANEL = 512
DECAY = 0.9
MESH = pl.DeviceIdType.MESH


def kernel(
    sections, ranks,
    acts, hidden, counts, momentum, act_grad,
    new_momentum, gram, received,
    x_buf, g_own, m_buf, xt_buf, g_in, nt_buf, own, send1, recv1, send2, recv2,
    load_sem, shift_send, shift_recv,
    g_send, g_recv, f_send, f_recv, s1_send, s1_recv, s2_send, s2_recv,
):
    section = lax.axis_index("pipe")
    expert_rank = lax.axis_index("expert")
    rank = lax.axis_index("tensor")
    pair = expert_rank // 2
    half = expert_rank % 2
    partner = {"expert": expert_rank + 1 - 2 * half}
    row_count, features = x_buf.shape
    rows, hidden_units = new_momentum.shape
    q, wide = send1.shape[2:]
    per_rank = g_own.shape[1] // wide
    share = row_count // 2
    first, last = section == 0, section == sections - 1

    if features == rows:
        x_src = acts.at[0, 0, :, pl.ds(pl.multiple_of(rank * rows, 128), rows)]
    else:
        x_src = acts.at[0, 0]
    load_x = pltpu.make_async_copy(x_src, x_buf, load_sem.at[0])
    load_g = pltpu.make_async_copy(hidden.at[0, pair], g_own, load_sem.at[1])
    load_m = pltpu.make_async_copy(momentum.at[0, 0], m_buf, load_sem.at[2])
    load_x.start()
    load_g.start()
    load_m.start()

    barrier = pltpu.get_barrier_semaphore()
    pl.semaphore_signal(barrier, inc=1, device_id=partner, device_id_type=MESH)
    for k in range(1, ranks):
        pl.semaphore_signal(
            barrier, inc=1, device_id={"tensor": (rank + k) % ranks}, device_id_type=MESH
        )

    @pl.when(jnp.logical_not(first))
    def _():
        pl.semaphore_signal(barrier, inc=1, device_id={"pipe": section - 1}, device_id_type=MESH)

    @pl.when(jnp.logical_not(last))
    def _():
        pl.semaphore_signal(barrier, inc=1, device_id={"pipe": section + 1}, device_id_type=MESH)

    ends = jnp.where(first, 1, 0) + jnp.where(last, 1, 0)
    pl.semaphore_wait(barrier, ranks + 2 - ends)

    shift = pltpu.make_async_remote_copy(
        src_ref=act_grad,
        dst_ref=received,
        send_sem=shift_send,
        recv_sem=shift_recv,
        device_id={"pipe": section - 1},
        device_id_type=MESH,
    )

    def clear_dead_rows():
        row = lax.broadcasted_iota(jnp.int32, (row_count, 1), 0)
        micro = counts.shape[2]
        block = row_count // micro
        limit = jnp.zeros((row_count, 1), jnp.int32)
        for b in range(micro):
            inside = jnp.logical_and(row >= b * block, row < (b + 1) * block)
            limit = jnp.where(inside, counts[0, pair, b] + b * block, limit)
        live = jnp.where(row < limit, 1.0, 0.0).astype(jnp.float32)
        masked = (x_buf[...].astype(jnp.float32) * live).astype(jnp.bfloat16)
        xt_buf[...] = masked.T

    def own_share(which):
        return pl.ds(pl.multiple_of(which * share, share), share)

    def as_rank(me):
        peers = [(me + k) % ranks for k in range(1, ranks)]

        def send_share(peer, c):
            return pltpu.make_async_remote_copy(
                src_ref=hidden.at[0, pair, own_share(half), pl.ds(c * wide, wide)],
                dst_ref=g_in.at[me, c, own_share(half)],
                send_sem=g_send.at[peer, c],
                recv_sem=g_recv.at[me, c],
                device_id={"tensor": peer},
                device_id_type=MESH,
            )

        def arrived_share(peer, c):
            place = g_in.at[peer, c, own_share(half)]
            return pltpu.make_async_remote_copy(
                src_ref=place,
                dst_ref=place,
                send_sem=g_send.at[peer, c],
                recv_sem=g_recv.at[peer, c],
                device_id={"tensor": peer},
                device_id_type=MESH,
            )

        def forward(peer, c, which):
            place = g_in.at[peer, c, own_share(which)]
            return pltpu.make_async_remote_copy(
                src_ref=place,
                dst_ref=place,
                send_sem=f_send.at[peer, c],
                recv_sem=f_recv.at[peer, c],
                device_id=partner,
                device_id_type=MESH,
            )

        def to_partner(owner, j):
            return pltpu.make_async_remote_copy(
                src_ref=send1.at[owner, j],
                dst_ref=recv1.at[owner, j],
                send_sem=s1_send.at[owner, j],
                recv_sem=s1_recv.at[owner, j],
                device_id=partner,
                device_id_type=MESH,
            )

        def to_rank(peer, slot, j):
            return pltpu.make_async_remote_copy(
                src_ref=send2.at[peer, j],
                dst_ref=recv2.at[slot, j],
                send_sem=s2_send.at[peer, j],
                recv_sem=s2_recv.at[slot, j],
                device_id={"tensor": peer},
                device_id_type=MESH,
            )

        for c in range(per_rank):
            for peer in peers:
                send_share(peer, c).start()

        @pl.when(jnp.logical_not(first))
        def _():
            shift.start()

        load_x.wait()
        clear_dead_rows()
        load_g.wait()
        load_m.wait()

        def update(j, gradients):
            cols = pl.ds(j * wide, wide)
            if features == rows:
                x_rows = xt_buf[...]
            else:
                x_rows = xt_buf[pl.ds(me * rows, rows), :]
            grad = jnp.dot(x_rows, gradients, preferred_element_type=jnp.float32)
            grad = grad.astype(jnp.bfloat16).astype(jnp.float32)
            new = (DECAY * m_buf[:, cols].astype(jnp.float32) + grad).astype(jnp.bfloat16)
            new_momentum[:, cols] = new
            if j < ranks:
                nt_buf[j] = new.T

        def piece(owner, j):
            sums = jnp.dot(
                nt_buf[owner],
                new_momentum[:, pl.ds(j * wide, wide)],
                preferred_element_type=jnp.float32,
            )
            top, bottom = sums[:q], sums[q:]
            own[owner, j] = jnp.where(half == 0, top, bottom)
            send1[owner, j] = jnp.where(half == 0, bottom, top).astype(jnp.bfloat16)
            to_partner(owner, j).start()

        def pass_on(owner, j):
            to_partner(owner, j).wait_recv()
            both = own[owner, j] + recv1[owner, j].astype(jnp.float32)
            send2[owner, j] = both.astype(jnp.bfloat16)
            to_rank(owner, me, j).start()

        ready, waiting = [], []

        def pieces(new):
            ready.extend(new)
            for owner in peers + [me]:
                if owner in ready:
                    for j in ready if owner in new else new:
                        piece(owner, j)
                        if owner != me:
                            waiting.append((owner, j))

        mine = [me * per_rank + c for c in range(per_rank)]
        for c in range(per_rank):
            update(mine[c], g_own[:, c * wide:(c + 1) * wide])
        pieces(mine)

        @pl.when(last)
        def _():
            received[...] = jnp.zeros_like(received)

        arrivals = [(peer, c) for c in range(per_rank) for peer in peers]
        for peer, c in arrivals:
            arrived_share(peer, c).wait_recv()
            forward(peer, c, half).start()
            while waiting:
                pass_on(*waiting.pop(0))
            forward(peer, c, 1 - half).wait_recv()
            update(peer * per_rank + c, g_in[peer, c])
            pieces([peer * per_rank + c])
        while waiting:
            pass_on(*waiting.pop(0))

        order = ready
        for j in order:
            to_partner(me, j).wait_recv()
            own[me, j] = own[me, j] + recv1[me, j].astype(jnp.float32)
        for j in order[per_rank:] + order[:per_rank]:
            total = own[me, j]
            for peer in peers:
                to_rank(peer, peer, j).wait_recv()
                total = total + recv2[peer, j].astype(jnp.float32)
            gram[:, pl.ds(j * wide, wide)] = total / D

        for peer, c in arrivals:
            send_share(peer, c).wait_send()
            forward(peer, c, half).wait_send()
        for j in order:
            for owner in peers + [me]:
                to_partner(owner, j).wait_send()
            for peer in peers:
                to_rank(peer, me, j).wait_send()

    for me in range(ranks):

        @pl.when(rank == me)
        def _():
            as_rank(me)

    @pl.when(jnp.logical_not(first))
    def _():
        shift.wait_send()

    @pl.when(jnp.logical_not(last))
    def _():
        shift.wait_recv()


def write_out(*refs):
    count = len(refs) // 2
    sems = refs[-1]
    copies = [
        pltpu.make_async_copy(refs[i], refs[count + i], sems.at[i]) for i in range(count)
    ]
    for copy in copies:
        copy.start()
    for copy in copies:
        copy.wait()


def on_device(acts, hidden_grad, counts, momentum, act_grad):
    sections, ranks = lax.axis_size("pipe"), lax.axis_size("tensor")
    row_count, features = acts.shape[2:]
    rows, units = momentum.shape[2:]
    width = hidden_grad.shape[3]
    q = PANEL // (2 * ranks)
    wide = 2 * q
    blocks = units // wide
    x_cols = rows if rows % 128 == 0 else features
    bf16, f32 = jnp.bfloat16, jnp.float32
    vmem, dma = pltpu.VMEM, pltpu.SemaphoreType.DMA
    hbm = pl.BlockSpec(memory_space=pltpu.HBM)
    anywhere = pl.BlockSpec(memory_space=pl.ANY)
    in_vmem = pl.BlockSpec(memory_space=vmem)

    def keep(x):
        return pltpu.with_memory_space_constraint(x, pltpu.HBM)

    results = pl.pallas_call(
        functools.partial(kernel, sections, ranks),
        out_shape=(
            vmem((rows, units), bf16),
            vmem((q, units), f32),
            vmem(act_grad.shape, bf16),
        ),
        in_specs=[hbm, hbm, pl.BlockSpec(memory_space=pltpu.SMEM), hbm, hbm],
        out_specs=(in_vmem, in_vmem, in_vmem),
        scratch_shapes=[
            vmem((row_count, x_cols), bf16),
            vmem((row_count, width), bf16),
            vmem((rows, units), bf16),
            vmem((x_cols, row_count), bf16),
            vmem((ranks, width // wide, row_count, wide), bf16),
            vmem((ranks, wide, rows), bf16),
            vmem((ranks, blocks, q, wide), f32),
            vmem((ranks, blocks, q, wide), bf16),
            vmem((ranks, blocks, q, wide), bf16),
            vmem((ranks, blocks, q, wide), bf16),
            vmem((ranks, blocks, q, wide), bf16),
            dma((3,)), dma, dma,
            dma((ranks, width // wide)), dma((ranks, width // wide)),
            dma((ranks, width // wide)), dma((ranks, width // wide)),
            dma((ranks, blocks)), dma((ranks, blocks)),
            dma((ranks, blocks)), dma((ranks, blocks)),
        ],
        compiler_params=pltpu.CompilerParams(
            collective_id=0, has_side_effects=True, vmem_limit_bytes=32 * 2**20
        ),
    )(keep(acts), keep(hidden_grad), keep(counts), keep(momentum), keep(act_grad))
    new_momentum, gram, received = pl.pallas_call(
        write_out,
        out_shape=tuple(pltpu.HBM(r.shape, r.dtype) for r in results),
        in_specs=[in_vmem] * 3,
        out_specs=(hbm,) * 3,
        scratch_shapes=[dma((3,))],
    )(*[pltpu.with_memory_space_constraint(r, vmem) for r in results])
    return (new_momentum[None, None], gram[None, None], received)


def solution(mesh):
    return jax.shard_map(
        on_device,
        mesh=mesh,
        in_specs=(
            P("pipe", "expert", None, None),
            P("pipe", None, None, "tensor"),
            P("pipe", None, None),
            P("pipe", "expert", "tensor", None),
            P("pipe", "expert", "tensor"),
        ),
        out_specs=(
            P("pipe", "expert", "tensor", None),
            P("pipe", "expert", "tensor", None),
            P("pipe", "expert", "tensor"),
        ),
        check_vma=False,
    )
```

```python
import functools

import jax
import jax.numpy as jnp
from jax import lax
from jax.experimental import pallas as pl
from jax.experimental.pallas import tpu as pltpu
from jax.sharding import PartitionSpec as P

D = 3584
PANEL = 512
DECAY = 0.9
MESH = pl.DeviceIdType.MESH


def kernel(
    sections, ranks,
    acts, hidden, counts, momentum, act_grad,
    new_momentum, gram, received,
    x_buf, g_own, m_buf, xt_buf, g_in, nt_buf, own, send1, recv1, send2, recv2,
    load_sem, shift_send, shift_recv,
    g_send, g_recv, f_send, f_recv, s1_send, s1_recv, s2_send, s2_recv,
):
    section = lax.axis_index("pipe")
    expert_rank = lax.axis_index("expert")
    rank = lax.axis_index("tensor")
    pair = expert_rank // 2
    half = expert_rank % 2
    partner = {"expert": expert_rank + 1 - 2 * half}
    row_count, features = x_buf.shape
    rows, hidden_units = new_momentum.shape
    q, wide = send1.shape[2:]
    per_rank = g_own.shape[1] // wide
    share = row_count // 2
    first, last = section == 0, section == sections - 1

    if features == rows:
        x_src = acts.at[0, 0, :, pl.ds(pl.multiple_of(rank * rows, 128), rows)]
    else:
        x_src = acts.at[0, 0]
    load_x = pltpu.make_async_copy(x_src, x_buf, load_sem.at[0])
    load_g = pltpu.make_async_copy(hidden.at[0, pair], g_own, load_sem.at[1])
    load_m = pltpu.make_async_copy(momentum.at[0, 0], m_buf, load_sem.at[2])
    load_g.start()
    load_x.start()
    load_m.start()

    barrier = pltpu.get_barrier_semaphore()
    pl.semaphore_signal(barrier, inc=1, device_id=partner, device_id_type=MESH)
    for k in range(1, ranks):
        pl.semaphore_signal(
            barrier, inc=1, device_id={"tensor": (rank + k) % ranks}, device_id_type=MESH
        )

    @pl.when(jnp.logical_not(first))
    def _():
        pl.semaphore_signal(barrier, inc=1, device_id={"pipe": section - 1}, device_id_type=MESH)

    @pl.when(jnp.logical_not(last))
    def _():
        pl.semaphore_signal(barrier, inc=1, device_id={"pipe": section + 1}, device_id_type=MESH)

    ends = jnp.where(first, 1, 0) + jnp.where(last, 1, 0)
    load_g.wait()
    pl.semaphore_wait(barrier, ranks + 2 - ends)

    shift = pltpu.make_async_remote_copy(
        src_ref=act_grad,
        dst_ref=received,
        send_sem=shift_send,
        recv_sem=shift_recv,
        device_id={"pipe": section - 1},
        device_id_type=MESH,
    )

    def clear_dead_rows():
        row = lax.broadcasted_iota(jnp.int32, (row_count, 1), 0)
        micro = counts.shape[2]
        block = row_count // micro
        limit = jnp.zeros((row_count, 1), jnp.int32)
        for b in range(micro):
            inside = jnp.logical_and(row >= b * block, row < (b + 1) * block)
            limit = jnp.where(inside, counts[0, pair, b] + b * block, limit)
        live = jnp.where(row < limit, 1.0, 0.0).astype(jnp.float32)
        masked = (x_buf[...].astype(jnp.float32) * live).astype(jnp.bfloat16)
        xt_buf[...] = masked.T

    def own_share(which):
        return pl.ds(pl.multiple_of(which * share, share), share)

    def as_rank(me):
        peers = [(me + k) % ranks for k in range(1, ranks)]

        def send_share(peer, c):
            return pltpu.make_async_remote_copy(
                src_ref=g_own.at[own_share(half), pl.ds(c * wide, wide)],
                dst_ref=g_in.at[me, c, own_share(half)],
                send_sem=g_send.at[peer, c],
                recv_sem=g_recv.at[me, c],
                device_id={"tensor": peer},
                device_id_type=MESH,
            )

        def arrived_share(peer, c):
            place = g_in.at[peer, c, own_share(half)]
            return pltpu.make_async_remote_copy(
                src_ref=place,
                dst_ref=place,
                send_sem=g_send.at[peer, c],
                recv_sem=g_recv.at[peer, c],
                device_id={"tensor": peer},
                device_id_type=MESH,
            )

        def forward(peer, c, which):
            place = g_in.at[peer, c, own_share(which)]
            return pltpu.make_async_remote_copy(
                src_ref=place,
                dst_ref=place,
                send_sem=f_send.at[peer, c],
                recv_sem=f_recv.at[peer, c],
                device_id=partner,
                device_id_type=MESH,
            )

        def to_partner(owner, j):
            return pltpu.make_async_remote_copy(
                src_ref=send1.at[owner, j],
                dst_ref=recv1.at[owner, j],
                send_sem=s1_send.at[owner, j],
                recv_sem=s1_recv.at[owner, j],
                device_id=partner,
                device_id_type=MESH,
            )

        def to_rank(peer, slot, j):
            return pltpu.make_async_remote_copy(
                src_ref=send2.at[peer, j],
                dst_ref=recv2.at[slot, j],
                send_sem=s2_send.at[peer, j],
                recv_sem=s2_recv.at[slot, j],
                device_id={"tensor": peer},
                device_id_type=MESH,
            )

        for c in range(per_rank):
            for peer in peers:
                send_share(peer, c).start()

        @pl.when(jnp.logical_not(first))
        def _():
            shift.start()

        load_x.wait()
        clear_dead_rows()
        load_m.wait()

        def update(j, gradients):
            cols = pl.ds(j * wide, wide)
            if features == rows:
                x_rows = xt_buf[...]
            else:
                x_rows = xt_buf[pl.ds(me * rows, rows), :]
            grad = jnp.dot(x_rows, gradients, preferred_element_type=jnp.float32)
            grad = grad.astype(jnp.bfloat16).astype(jnp.float32)
            new = (DECAY * m_buf[:, cols].astype(jnp.float32) + grad).astype(jnp.bfloat16)
            new_momentum[:, cols] = new
            if j < ranks:
                nt_buf[j] = new.T

        def piece(owner, j):
            sums = jnp.dot(
                nt_buf[owner],
                new_momentum[:, pl.ds(j * wide, wide)],
                preferred_element_type=jnp.float32,
            )
            top, bottom = sums[:q], sums[q:]
            own[owner, j] = jnp.where(half == 0, top, bottom)
            send1[owner, j] = jnp.where(half == 0, bottom, top).astype(jnp.bfloat16)
            to_partner(owner, j).start()

        def pass_on(owner, j):
            to_partner(owner, j).wait_recv()
            both = own[owner, j] + recv1[owner, j].astype(jnp.float32)
            send2[owner, j] = both.astype(jnp.bfloat16)
            to_rank(owner, me, j).start()

        arrivals = [(peer, c) for c in range(per_rank) for peer in peers]
        coming = list(arrivals)

        def forward_next():
            if coming:
                peer, c = coming.pop(0)
                arrived_share(peer, c).wait_recv()
                forward(peer, c, half).start()

        ready, waiting = [], []

        def pieces(new, forward_after):
            ready.extend(new)
            todo = [
                (owner, j)
                for owner in peers + [me]
                if owner in ready
                for j in (ready if owner in new else new)
            ]
            for n, (owner, j) in enumerate(todo):
                piece(owner, j)
                if n in forward_after:
                    forward_next()
                waiting[:] = [(owner, j, age + 1) for owner, j, age in waiting]
                while waiting and waiting[0][2] >= 2:
                    pass_on(*waiting.pop(0)[:2])
                if owner != me:
                    waiting.append((owner, j, 0))
            return bool(todo)

        mine = [me * per_rank + c for c in range(per_rank)]
        for c in range(per_rank):
            update(mine[c], g_own[:, c * wide:(c + 1) * wide])
        busy = pieces(mine, (1, 3))
        if not busy:
            forward_next()

        @pl.when(last)
        def _():
            received[...] = jnp.zeros_like(received)

        for peer, c in arrivals:
            if (peer, c) in coming:
                forward_next()
            forward(peer, c, 1 - half).wait_recv()
            update(peer * per_rank + c, g_in[peer, c])
            pieces([peer * per_rank + c], (0,))
        while waiting:
            pass_on(*waiting.pop(0)[:2])

        order = ready
        for j in order:
            to_partner(me, j).wait_recv()
            own[me, j] = own[me, j] + recv1[me, j].astype(jnp.float32)
        for j in order[per_rank:] + order[:per_rank]:
            total = own[me, j]
            for peer in peers:
                to_rank(peer, peer, j).wait_recv()
                total = total + recv2[peer, j].astype(jnp.float32)
            gram[:, pl.ds(j * wide, wide)] = total / D

        for peer, c in arrivals:
            send_share(peer, c).wait_send()
            forward(peer, c, half).wait_send()
        for j in order:
            for owner in peers + [me]:
                to_partner(owner, j).wait_send()
            for peer in peers:
                to_rank(peer, me, j).wait_send()

    for me in range(ranks):

        @pl.when(rank == me)
        def _():
            as_rank(me)

    @pl.when(jnp.logical_not(first))
    def _():
        shift.wait_send()

    @pl.when(jnp.logical_not(last))
    def _():
        shift.wait_recv()


def write_out(cuts, *refs):
    count = len(cuts)
    sems = refs[-1]
    copies = []
    for i, cut in enumerate(cuts):
        rows = refs[i].shape[-2] // cut
        for n in range(cut):
            place = (slice(None),) * (len(refs[i].shape) - 2) + (pl.ds(n * rows, rows),)
            copies.append(
                pltpu.make_async_copy(
                    refs[i].at[place], refs[count + i].at[place], sems.at[len(copies)]
                )
            )
    for copy in copies:
        copy.start()
    for copy in copies:
        copy.wait()


def on_device(acts, hidden_grad, counts, momentum, act_grad):
    sections, ranks = lax.axis_size("pipe"), lax.axis_size("tensor")
    row_count, features = acts.shape[2:]
    rows, units = momentum.shape[2:]
    width = hidden_grad.shape[3]
    q = PANEL // (2 * ranks)
    wide = 2 * q
    blocks = units // wide
    x_cols = rows if rows % 128 == 0 else features
    bf16, f32 = jnp.bfloat16, jnp.float32
    vmem, dma = pltpu.VMEM, pltpu.SemaphoreType.DMA
    hbm = pl.BlockSpec(memory_space=pltpu.HBM)
    anywhere = pl.BlockSpec(memory_space=pl.ANY)
    in_vmem = pl.BlockSpec(memory_space=vmem)

    def keep(x):
        return pltpu.with_memory_space_constraint(x, pltpu.HBM)

    results = pl.pallas_call(
        functools.partial(kernel, sections, ranks),
        out_shape=(
            vmem((rows, units), bf16),
            vmem((q, units), f32),
            vmem(act_grad.shape, bf16),
        ),
        in_specs=[hbm, hbm, pl.BlockSpec(memory_space=pltpu.SMEM), hbm, hbm],
        out_specs=(in_vmem, in_vmem, in_vmem),
        scratch_shapes=[
            vmem((row_count, x_cols), bf16),
            vmem((row_count, width), bf16),
            vmem((rows, units), bf16),
            vmem((x_cols, row_count), bf16),
            vmem((ranks, width // wide, row_count, wide), bf16),
            vmem((ranks, wide, rows), bf16),
            vmem((ranks, blocks, q, wide), f32),
            vmem((ranks, blocks, q, wide), bf16),
            vmem((ranks, blocks, q, wide), bf16),
            vmem((ranks, blocks, q, wide), bf16),
            vmem((ranks, blocks, q, wide), bf16),
            dma((3,)), dma, dma,
            dma((ranks, width // wide)), dma((ranks, width // wide)),
            dma((ranks, width // wide)), dma((ranks, width // wide)),
            dma((ranks, blocks)), dma((ranks, blocks)),
            dma((ranks, blocks)), dma((ranks, blocks)),
        ],
        compiler_params=pltpu.CompilerParams(
            collective_id=0, has_side_effects=True, vmem_limit_bytes=32 * 2**20
        ),
    )(keep(acts), keep(hidden_grad), keep(counts), keep(momentum), keep(act_grad))
    new_momentum, gram, received = pl.pallas_call(
        functools.partial(write_out, (4, 2, 2)),
        out_shape=tuple(pltpu.HBM(r.shape, r.dtype) for r in results),
        in_specs=[in_vmem] * 3,
        out_specs=(hbm,) * 3,
        scratch_shapes=[dma((8,))],
    )(*[pltpu.with_memory_space_constraint(r, vmem) for r in results])
    return (new_momentum[None, None], gram[None, None], received)


def solution(mesh):
    return jax.shard_map(
        on_device,
        mesh=mesh,
        in_specs=(
            P("pipe", "expert", None, None),
            P("pipe", None, None, "tensor"),
            P("pipe", None, None),
            P("pipe", "expert", "tensor", None),
            P("pipe", "expert", "tensor"),
        ),
        out_specs=(
            P("pipe", "expert", "tensor", None),
            P("pipe", "expert", "tensor", None),
            P("pipe", "expert", "tensor"),
        ),
        check_vma=False,
    )
```

```python
import functools

import jax
import jax.numpy as jnp
from jax import lax
from jax.experimental import pallas as pl
from jax.experimental.pallas import tpu as pltpu
from jax.sharding import PartitionSpec as P

D = 3584
PANEL = 512
DECAY = 0.9
MESH = pl.DeviceIdType.MESH


def kernel(
    sections, ranks,
    acts, hidden, counts_in, momentum, act_grad,
    new_momentum, gram, received,
    counts, x_buf, g_own, m_buf, xt_buf, g_in, nt_buf, own, send1, recv1, send2, recv2,
    load_sem, shift_send, shift_recv,
    g_send, g_recv, f_send, f_recv, s1_send, s1_recv, s2_send, s2_recv,
):
    section = lax.axis_index("pipe")
    expert_rank = lax.axis_index("expert")
    rank = lax.axis_index("tensor")
    pair = expert_rank // 2
    half = expert_rank % 2
    partner = {"expert": expert_rank + 1 - 2 * half}
    row_count, features = x_buf.shape
    rows, hidden_units = new_momentum.shape
    q, wide = send1.shape[2:]
    per_rank = g_own.shape[1] // wide
    share = row_count // 2
    first, last = section == 0, section == sections - 1

    if features == rows:
        x_src = acts.at[0, 0, :, pl.ds(pl.multiple_of(rank * rows, 128), rows)]
    else:
        x_src = acts.at[0, 0]
    load_x = pltpu.make_async_copy(x_src, x_buf, load_sem.at[0])
    load_g = pltpu.make_async_copy(hidden.at[0, pair], g_own, load_sem.at[1])
    load_m = pltpu.make_async_copy(momentum.at[0, 0], m_buf, load_sem.at[2])
    load_counts = pltpu.make_async_copy(counts_in, counts, load_sem.at[3])
    load_g.start()

    barrier = pltpu.get_barrier_semaphore()
    pl.semaphore_signal(barrier, inc=1, device_id=partner, device_id_type=MESH)
    for k in range(1, ranks):
        pl.semaphore_signal(
            barrier, inc=1, device_id={"tensor": (rank + k) % ranks}, device_id_type=MESH
        )

    @pl.when(jnp.logical_not(first))
    def _():
        pl.semaphore_signal(barrier, inc=1, device_id={"pipe": section - 1}, device_id_type=MESH)

    @pl.when(jnp.logical_not(last))
    def _():
        pl.semaphore_signal(barrier, inc=1, device_id={"pipe": section + 1}, device_id_type=MESH)

    ends = jnp.where(first, 1, 0) + jnp.where(last, 1, 0)
    load_x.start()
    load_counts.start()
    load_m.start()
    load_g.wait()
    pl.semaphore_wait(barrier, ranks + 2 - ends)

    shift = pltpu.make_async_remote_copy(
        src_ref=act_grad,
        dst_ref=received,
        send_sem=shift_send,
        recv_sem=shift_recv,
        device_id={"pipe": section - 1},
        device_id_type=MESH,
    )

    def clear_dead_rows():
        row = lax.broadcasted_iota(jnp.int32, (row_count, 1), 0)
        micro = counts.shape[2]
        block = row_count // micro
        limit = jnp.zeros((row_count, 1), jnp.int32)
        for b in range(micro):
            inside = jnp.logical_and(row >= b * block, row < (b + 1) * block)
            limit = jnp.where(inside, counts[0, pair, b] + b * block, limit)
        live = jnp.where(row < limit, 1.0, 0.0).astype(jnp.float32)
        masked = (x_buf[...].astype(jnp.float32) * live).astype(jnp.bfloat16)
        xt_buf[...] = masked.T

    def own_share(which):
        return pl.ds(pl.multiple_of(which * share, share), share)

    def as_rank(me):
        peers = [(me + k) % ranks for k in range(1, ranks)]

        def send_share(peer, c):
            return pltpu.make_async_remote_copy(
                src_ref=g_own.at[own_share(half), pl.ds(c * wide, wide)],
                dst_ref=g_in.at[me, c, own_share(half)],
                send_sem=g_send.at[peer, c],
                recv_sem=g_recv.at[me, c],
                device_id={"tensor": peer},
                device_id_type=MESH,
            )

        def arrived_share(peer, c):
            place = g_in.at[peer, c, own_share(half)]
            return pltpu.make_async_remote_copy(
                src_ref=place,
                dst_ref=place,
                send_sem=g_send.at[peer, c],
                recv_sem=g_recv.at[peer, c],
                device_id={"tensor": peer},
                device_id_type=MESH,
            )

        def forward(peer, c, which):
            place = g_in.at[peer, c, own_share(which)]
            return pltpu.make_async_remote_copy(
                src_ref=place,
                dst_ref=place,
                send_sem=f_send.at[peer, c],
                recv_sem=f_recv.at[peer, c],
                device_id=partner,
                device_id_type=MESH,
            )

        def to_partner(owner, j):
            return pltpu.make_async_remote_copy(
                src_ref=send1.at[owner, j],
                dst_ref=recv1.at[owner, j],
                send_sem=s1_send.at[owner, j],
                recv_sem=s1_recv.at[owner, j],
                device_id=partner,
                device_id_type=MESH,
            )

        def to_rank(peer, slot, j):
            return pltpu.make_async_remote_copy(
                src_ref=send2.at[peer, j],
                dst_ref=recv2.at[slot, j],
                send_sem=s2_send.at[peer, j],
                recv_sem=s2_recv.at[slot, j],
                device_id={"tensor": peer},
                device_id_type=MESH,
            )

        for c in range(per_rank):
            for peer in peers:
                send_share(peer, c).start()

        @pl.when(jnp.logical_not(first))
        def _():
            shift.start()

        load_x.wait()
        load_counts.wait()
        clear_dead_rows()
        load_m.wait()

        def update(j, gradients):
            cols = pl.ds(j * wide, wide)
            if features == rows:
                x_rows = xt_buf[...]
            else:
                x_rows = xt_buf[pl.ds(me * rows, rows), :]
            grad = jnp.dot(x_rows, gradients, preferred_element_type=jnp.float32)
            grad = grad.astype(jnp.bfloat16).astype(jnp.float32)
            new = (DECAY * m_buf[:, cols].astype(jnp.float32) + grad).astype(jnp.bfloat16)
            new_momentum[:, cols] = new
            if j < ranks:
                nt_buf[j] = new.T

        def piece(owner, j):
            sums = jnp.dot(
                nt_buf[owner],
                new_momentum[:, pl.ds(j * wide, wide)],
                preferred_element_type=jnp.float32,
            )
            top, bottom = sums[:q], sums[q:]
            own[owner, j] = jnp.where(half == 0, top, bottom)
            send1[owner, j] = jnp.where(half == 0, bottom, top).astype(jnp.bfloat16)
            to_partner(owner, j).start()

        def pass_on(owner, j):
            to_partner(owner, j).wait_recv()
            both = own[owner, j] + recv1[owner, j].astype(jnp.float32)
            send2[owner, j] = both.astype(jnp.bfloat16)
            to_rank(owner, me, j).start()

        arrivals = [(peer, c) for c in range(per_rank) for peer in peers]
        coming = list(arrivals)

        def forward_next():
            if coming:
                peer, c = coming.pop(0)
                arrived_share(peer, c).wait_recv()
                forward(peer, c, half).start()

        ready, waiting = [], []

        def pieces(new, forward_after):
            ready.extend(new)
            todo = [
                (owner, j)
                for owner in peers + [me]
                if owner in ready
                for j in (ready if owner in new else new)
            ]
            for n, (owner, j) in enumerate(todo):
                piece(owner, j)
                if n in forward_after:
                    forward_next()
                waiting[:] = [(owner, j, age + 1) for owner, j, age in waiting]
                while waiting and waiting[0][2] >= 2:
                    pass_on(*waiting.pop(0)[:2])
                if owner != me:
                    waiting.append((owner, j, 0))
            return bool(todo)

        mine = [me * per_rank + c for c in range(per_rank)]
        for c in range(per_rank):
            update(mine[c], g_own[:, c * wide:(c + 1) * wide])
        busy = pieces(mine, (1, 3))
        if not busy:
            forward_next()

        @pl.when(last)
        def _():
            received[...] = jnp.zeros_like(received)

        for peer, c in arrivals:
            if (peer, c) in coming:
                forward_next()
            forward(peer, c, 1 - half).wait_recv()
            update(peer * per_rank + c, g_in[peer, c])
            pieces([peer * per_rank + c], (0,))
        while waiting:
            pass_on(*waiting.pop(0)[:2])

        order = ready
        for j in order:
            to_partner(me, j).wait_recv()
            own[me, j] = own[me, j] + recv1[me, j].astype(jnp.float32)
        for j in order[per_rank:] + order[:per_rank]:
            total = own[me, j]
            for peer in peers:
                to_rank(peer, peer, j).wait_recv()
                total = total + recv2[peer, j].astype(jnp.float32)
            gram[:, pl.ds(j * wide, wide)] = total / D

        for peer, c in arrivals:
            send_share(peer, c).wait_send()
            forward(peer, c, half).wait_send()
        for j in order:
            for owner in peers + [me]:
                to_partner(owner, j).wait_send()
            for peer in peers:
                to_rank(peer, me, j).wait_send()

    for me in range(ranks):

        @pl.when(rank == me)
        def _():
            as_rank(me)

    @pl.when(jnp.logical_not(first))
    def _():
        shift.wait_send()

    @pl.when(jnp.logical_not(last))
    def _():
        shift.wait_recv()


def write_out(cuts, *refs):
    count = len(cuts)
    sems = refs[-1]
    copies = []
    for i, cut in enumerate(cuts):
        rows = refs[i].shape[-2] // cut
        for n in range(cut):
            place = (slice(None),) * (len(refs[i].shape) - 2) + (pl.ds(n * rows, rows),)
            copies.append(
                pltpu.make_async_copy(
                    refs[i].at[place], refs[count + i].at[place], sems.at[len(copies)]
                )
            )
    for copy in copies:
        copy.start()
    for copy in copies:
        copy.wait()


def on_device(acts, hidden_grad, counts, momentum, act_grad):
    sections, ranks = lax.axis_size("pipe"), lax.axis_size("tensor")
    row_count, features = acts.shape[2:]
    rows, units = momentum.shape[2:]
    width = hidden_grad.shape[3]
    q = PANEL // (2 * ranks)
    wide = 2 * q
    blocks = units // wide
    x_cols = rows if rows % 128 == 0 else features
    bf16, f32 = jnp.bfloat16, jnp.float32
    vmem, dma = pltpu.VMEM, pltpu.SemaphoreType.DMA
    hbm = pl.BlockSpec(memory_space=pltpu.HBM)
    anywhere = pl.BlockSpec(memory_space=pl.ANY)
    in_vmem = pl.BlockSpec(memory_space=vmem)

    def keep(x):
        return pltpu.with_memory_space_constraint(x, pltpu.HBM)

    results = pl.pallas_call(
        functools.partial(kernel, sections, ranks),
        out_shape=(
            vmem((rows, units), bf16),
            vmem((q, units), f32),
            vmem(act_grad.shape, bf16),
        ),
        in_specs=[hbm] * 5,
        out_specs=(in_vmem, in_vmem, in_vmem),
        scratch_shapes=[
            pltpu.SMEM(counts.shape, counts.dtype),
            vmem((row_count, x_cols), bf16),
            vmem((row_count, width), bf16),
            vmem((rows, units), bf16),
            vmem((x_cols, row_count), bf16),
            vmem((ranks, width // wide, row_count, wide), bf16),
            vmem((ranks, wide, rows), bf16),
            vmem((ranks, blocks, q, wide), f32),
            vmem((ranks, blocks, q, wide), bf16),
            vmem((ranks, blocks, q, wide), bf16),
            vmem((ranks, blocks, q, wide), bf16),
            vmem((ranks, blocks, q, wide), bf16),
            dma((4,)), dma, dma,
            dma((ranks, width // wide)), dma((ranks, width // wide)),
            dma((ranks, width // wide)), dma((ranks, width // wide)),
            dma((ranks, blocks)), dma((ranks, blocks)),
            dma((ranks, blocks)), dma((ranks, blocks)),
        ],
        compiler_params=pltpu.CompilerParams(
            collective_id=0, has_side_effects=True, vmem_limit_bytes=32 * 2**20
        ),
    )(keep(acts), keep(hidden_grad), keep(counts), keep(momentum), keep(act_grad))
    new_momentum, gram, received = pl.pallas_call(
        functools.partial(write_out, (4, 2, 2)),
        out_shape=tuple(pltpu.HBM(r.shape, r.dtype) for r in results),
        in_specs=[in_vmem] * 3,
        out_specs=(hbm,) * 3,
        scratch_shapes=[dma((8,))],
    )(*[pltpu.with_memory_space_constraint(r, vmem) for r in results])
    return (new_momentum[None, None], gram[None, None], received)


def solution(mesh):
    return jax.shard_map(
        on_device,
        mesh=mesh,
        in_specs=(
            P("pipe", "expert", None, None),
            P("pipe", None, None, "tensor"),
            P("pipe", None, None),
            P("pipe", "expert", "tensor", None),
            P("pipe", "expert", "tensor"),
        ),
        out_specs=(
            P("pipe", "expert", "tensor", None),
            P("pipe", "expert", "tensor", None),
            P("pipe", "expert", "tensor"),
        ),
        check_vma=False,
    )
```

```python
import functools

import jax
import jax.numpy as jnp
from jax import lax
from jax.experimental import pallas as pl
from jax.experimental.pallas import tpu as pltpu
from jax.sharding import PartitionSpec as P

D = 3584
PANEL = 512
DECAY = 0.9
MESH = pl.DeviceIdType.MESH


def kernel(
    sections, ranks,
    acts, hidden, counts_in, momentum, act_grad,
    new_momentum, gram, received,
    counts, x_buf, g_own, m_buf, xt_buf, g_in, nt_buf, own, send1, recv1, send2, recv2,
    load_sem, shift_send, shift_recv,
    d_send, d_recv, g_send, g_recv, f_send, f_recv, s1_send, s1_recv, s2_send, s2_recv,
):
    section = lax.axis_index("pipe")
    expert_rank = lax.axis_index("expert")
    rank = lax.axis_index("tensor")
    pair = expert_rank // 2
    half = expert_rank % 2
    other_half = expert_rank + 1 - 2 * half
    partner = {"expert": other_half}
    row_count, features = x_buf.shape
    rows, hidden_units = new_momentum.shape
    q, wide = send1.shape[2:]
    per_rank = g_own.shape[1] // wide
    share = row_count // 2
    subs = 2 if q % 128 == 0 else 1
    thin = wide // subs
    first, last = section == 0, section == sections - 1

    if features == rows:
        x_src = acts.at[0, 0, :, pl.ds(pl.multiple_of(rank * rows, 128), rows)]
    else:
        x_src = acts.at[0, 0]
    load_x = pltpu.make_async_copy(x_src, x_buf, load_sem.at[0])
    load_g = pltpu.make_async_copy(hidden.at[0, pair], g_own, load_sem.at[1])
    load_m = pltpu.make_async_copy(momentum.at[0, 0], m_buf, load_sem.at[2])
    load_counts = pltpu.make_async_copy(counts_in, counts, load_sem.at[3])
    load_g.start()

    barrier = pltpu.get_barrier_semaphore()
    pl.semaphore_signal(barrier, inc=1, device_id=partner, device_id_type=MESH)
    for k in range(1, ranks):
        pl.semaphore_signal(
            barrier, inc=1, device_id={"tensor": (rank + k) % ranks}, device_id_type=MESH
        )
        pl.semaphore_signal(
            barrier,
            inc=1,
            device_id={"expert": other_half, "tensor": (rank + k) % ranks},
            device_id_type=MESH,
        )

    @pl.when(jnp.logical_not(first))
    def _():
        pl.semaphore_signal(barrier, inc=1, device_id={"pipe": section - 1}, device_id_type=MESH)

    @pl.when(jnp.logical_not(last))
    def _():
        pl.semaphore_signal(barrier, inc=1, device_id={"pipe": section + 1}, device_id_type=MESH)

    ends = jnp.where(first, 1, 0) + jnp.where(last, 1, 0)
    load_x.start()
    load_counts.start()
    load_m.start()
    load_g.wait()
    pl.semaphore_wait(barrier, 2 * ranks + 1 - ends)

    shift = pltpu.make_async_remote_copy(
        src_ref=act_grad,
        dst_ref=received,
        send_sem=shift_send,
        recv_sem=shift_recv,
        device_id={"pipe": section - 1},
        device_id_type=MESH,
    )

    def clear_dead_rows():
        row = lax.broadcasted_iota(jnp.int32, (row_count, 1), 0)
        micro = counts.shape[2]
        block = row_count // micro
        limit = jnp.zeros((row_count, 1), jnp.int32)
        for b in range(micro):
            inside = jnp.logical_and(row >= b * block, row < (b + 1) * block)
            limit = jnp.where(inside, counts[0, pair, b] + b * block, limit)
        live = jnp.where(row < limit, 1.0, 0.0).astype(jnp.float32)
        masked = (x_buf[...].astype(jnp.float32) * live).astype(jnp.bfloat16)
        xt_buf[...] = masked.T

    def own_share(which):
        return pl.ds(pl.multiple_of(which * share, share), share)

    def as_rank(me):
        peers = [(me + k) % ranks for k in range(1, ranks)]

        def send_share(peer, c):
            return pltpu.make_async_remote_copy(
                src_ref=g_own.at[own_share(half), pl.ds(c * wide, wide)],
                dst_ref=g_in.at[me, c, own_share(half)],
                send_sem=g_send.at[peer, c],
                recv_sem=g_recv.at[me, c],
                device_id={"tensor": peer},
                device_id_type=MESH,
            )

        def arrived_share(peer, c):
            place = g_in.at[peer, c, own_share(half)]
            return pltpu.make_async_remote_copy(
                src_ref=place,
                dst_ref=place,
                send_sem=g_send.at[peer, c],
                recv_sem=g_recv.at[peer, c],
                device_id={"tensor": peer},
                device_id_type=MESH,
            )

        def forward(peer, c, which):
            place = g_in.at[peer, c, own_share(which)]
            return pltpu.make_async_remote_copy(
                src_ref=place,
                dst_ref=place,
                send_sem=f_send.at[peer, c],
                recv_sem=f_recv.at[peer, c],
                device_id=partner,
                device_id_type=MESH,
            )

        def direct(peer, c):
            return c == 0 and peer * per_rank < ranks

        def send_direct(peer, away, sub):
            target = {"tensor": peer}
            if away:
                target["expert"] = other_half
            cols = pl.ds(sub * thin, thin)
            return pltpu.make_async_remote_copy(
                src_ref=g_own.at[own_share(half), cols],
                dst_ref=g_in.at[me, 0, own_share(half), cols],
                send_sem=d_send.at[peer, away, sub],
                recv_sem=d_recv.at[me, away, sub],
                device_id=target,
                device_id_type=MESH,
            )

        def arrived_direct(peer, away, sub):
            which = 1 - half if away else half
            place = g_in.at[peer, 0, own_share(which), pl.ds(sub * thin, thin)]
            return pltpu.make_async_remote_copy(
                src_ref=place,
                dst_ref=place,
                send_sem=d_send.at[peer, away, sub],
                recv_sem=d_recv.at[peer, away, sub],
                device_id={"tensor": peer},
                device_id_type=MESH,
            )

        def to_partner(owner, j):
            return pltpu.make_async_remote_copy(
                src_ref=send1.at[owner, j],
                dst_ref=recv1.at[owner, j],
                send_sem=s1_send.at[owner, j],
                recv_sem=s1_recv.at[owner, j],
                device_id=partner,
                device_id_type=MESH,
            )

        def to_rank(peer, slot, j):
            return pltpu.make_async_remote_copy(
                src_ref=send2.at[peer, j],
                dst_ref=recv2.at[slot, j],
                send_sem=s2_send.at[peer, j],
                recv_sem=s2_recv.at[slot, j],
                device_id={"tensor": peer},
                device_id_type=MESH,
            )

        for c in range(per_rank):
            if direct(me, c):
                for sub in range(subs):
                    for peer in peers:
                        for away in range(2):
                            send_direct(peer, away, sub).start()
            else:
                for peer in peers:
                    send_share(peer, c).start()

        @pl.when(jnp.logical_not(first))
        def _():
            shift.start()

        load_x.wait()
        load_counts.wait()
        clear_dead_rows()
        load_m.wait()

        def update(j, gradients, at=0):
            size = gradients.shape[1]
            cols = pl.ds(j * wide + at, size)
            if features == rows:
                x_rows = xt_buf[...]
            else:
                x_rows = xt_buf[pl.ds(me * rows, rows), :]
            grad = jnp.dot(x_rows, gradients, preferred_element_type=jnp.float32)
            grad = grad.astype(jnp.bfloat16).astype(jnp.float32)
            new = (DECAY * m_buf[:, cols].astype(jnp.float32) + grad).astype(jnp.bfloat16)
            new_momentum[:, cols] = new
            if j < ranks:
                nt_buf[j, pl.ds(at, size)] = new.T

        def piece(owner, j):
            sums = jnp.dot(
                nt_buf[owner],
                new_momentum[:, pl.ds(j * wide, wide)],
                preferred_element_type=jnp.float32,
            )
            top, bottom = sums[:q], sums[q:]
            own[owner, j] = jnp.where(half == 0, top, bottom)
            send1[owner, j] = jnp.where(half == 0, bottom, top).astype(jnp.bfloat16)
            to_partner(owner, j).start()

        def half_piece(owner, j, keeper):
            sums = jnp.dot(
                nt_buf[owner, pl.ds(keeper * q, q)],
                new_momentum[:, pl.ds(j * wide, wide)],
                preferred_element_type=jnp.float32,
            )

            @pl.when(half == keeper)
            def _():
                own[owner, j] = sums

            @pl.when(half != keeper)
            def _():
                send1[owner, j] = sums.astype(jnp.bfloat16)
                to_partner(owner, j).start()

        def pass_on(owner, j):
            to_partner(owner, j).wait_recv()
            both = own[owner, j] + recv1[owner, j].astype(jnp.float32)
            send2[owner, j] = both.astype(jnp.bfloat16)
            to_rank(owner, me, j).start()

        arrivals = [(peer, c) for c in range(per_rank) for peer in peers]
        coming = [a for a in arrivals if not direct(*a)]

        def forward_next():
            if coming:
                peer, c = coming.pop(0)
                arrived_share(peer, c).wait_recv()
                forward(peer, c, half).start()

        ready, waiting = [], []

        def pieces(new, forward_after, done=()):
            ready.extend(new)
            todo = [
                (owner, j)
                for owner in peers + [me]
                if owner in ready
                for j in (ready if owner in new else new)
                if (owner, j) not in done
            ]
            for n, (owner, j) in enumerate(todo):
                piece(owner, j)
                if n in forward_after:
                    forward_next()
                waiting[:] = [(owner, j, age + 1) for owner, j, age in waiting]
                while waiting and waiting[0][2] >= 2:
                    pass_on(*waiting.pop(0)[:2])
                if owner != me:
                    waiting.append((owner, j, 0))

        mine = [me * per_rank + c for c in range(per_rank)]
        for c in range(per_rank):
            update(mine[c], g_own[:, c * wide:(c + 1) * wide])
        pieces(mine, (1, 3))

        @pl.when(last)
        def _():
            received[...] = jnp.zeros_like(received)

        for peer, c in arrivals:
            j = peer * per_rank + c
            if direct(peer, c):
                before = list(ready)
                for sub in range(subs):
                    for away in range(2):
                        arrived_direct(peer, away, sub).wait_recv()
                    update(j, g_in[peer, c, :, pl.ds(sub * thin, thin)], sub * thin)
                    if subs == 2:
                        for i in before:
                            half_piece(j, i, sub)
                done = [(j, i) for i in before] if subs == 2 else []
                if done and j != me:

                    @pl.when(half == 0)
                    def _():
                        for item in done:
                            pass_on(*item)

                pieces([j], (0,), done)
                if done and j != me:

                    @pl.when(half == 1)
                    def _():
                        for item in done:
                            pass_on(*item)

                continue
            if (peer, c) in coming:
                forward_next()
            forward(peer, c, 1 - half).wait_recv()
            update(j, g_in[peer, c])
            pieces([j], (0,))
        while waiting:
            pass_on(*waiting.pop(0)[:2])

        order = ready
        for j in order:
            to_partner(me, j).wait_recv()
            own[me, j] = own[me, j] + recv1[me, j].astype(jnp.float32)
        for j in order[per_rank:] + order[:per_rank]:
            total = own[me, j]
            for peer in peers:
                to_rank(peer, peer, j).wait_recv()
                total = total + recv2[peer, j].astype(jnp.float32)
            gram[:, pl.ds(j * wide, wide)] = total / D

        for peer, c in arrivals:
            if direct(me, c):
                for sub in range(subs):
                    for away in range(2):
                        send_direct(peer, away, sub).wait_send()
            else:
                send_share(peer, c).wait_send()
            if not direct(peer, c):
                forward(peer, c, half).wait_send()
        for j in order:
            for owner in peers + [me]:
                to_partner(owner, j).wait_send()
            for peer in peers:
                to_rank(peer, me, j).wait_send()

    for me in range(ranks):

        @pl.when(rank == me)
        def _():
            as_rank(me)

    @pl.when(jnp.logical_not(first))
    def _():
        shift.wait_send()

    @pl.when(jnp.logical_not(last))
    def _():
        shift.wait_recv()


def write_out(cuts, *refs):
    count = len(cuts)
    sems = refs[-1]
    copies = []
    for i, cut in enumerate(cuts):
        rows = refs[i].shape[-2] // cut
        for n in range(cut):
            place = (slice(None),) * (len(refs[i].shape) - 2) + (pl.ds(n * rows, rows),)
            copies.append(
                pltpu.make_async_copy(
                    refs[i].at[place], refs[count + i].at[place], sems.at[len(copies)]
                )
            )
    for copy in copies:
        copy.start()
    for copy in copies:
        copy.wait()


def on_device(acts, hidden_grad, counts, momentum, act_grad):
    sections, ranks = lax.axis_size("pipe"), lax.axis_size("tensor")
    row_count, features = acts.shape[2:]
    rows, units = momentum.shape[2:]
    width = hidden_grad.shape[3]
    q = PANEL // (2 * ranks)
    wide = 2 * q
    blocks = units // wide
    x_cols = rows if rows % 128 == 0 else features
    bf16, f32 = jnp.bfloat16, jnp.float32
    vmem, dma = pltpu.VMEM, pltpu.SemaphoreType.DMA
    hbm = pl.BlockSpec(memory_space=pltpu.HBM)
    anywhere = pl.BlockSpec(memory_space=pl.ANY)
    in_vmem = pl.BlockSpec(memory_space=vmem)

    def keep(x):
        return pltpu.with_memory_space_constraint(x, pltpu.HBM)

    results = pl.pallas_call(
        functools.partial(kernel, sections, ranks),
        out_shape=(
            vmem((rows, units), bf16),
            vmem((q, units), f32),
            vmem(act_grad.shape, bf16),
        ),
        in_specs=[hbm] * 5,
        out_specs=(in_vmem, in_vmem, in_vmem),
        scratch_shapes=[
            pltpu.SMEM(counts.shape, counts.dtype),
            vmem((row_count, x_cols), bf16),
            vmem((row_count, width), bf16),
            vmem((rows, units), bf16),
            vmem((x_cols, row_count), bf16),
            vmem((ranks, width // wide, row_count, wide), bf16),
            vmem((ranks, wide, rows), bf16),
            vmem((ranks, blocks, q, wide), f32),
            vmem((ranks, blocks, q, wide), bf16),
            vmem((ranks, blocks, q, wide), bf16),
            vmem((ranks, blocks, q, wide), bf16),
            vmem((ranks, blocks, q, wide), bf16),
            dma((4,)), dma, dma,
            dma((ranks, 2, 2)), dma((ranks, 2, 2)),
            dma((ranks, width // wide)), dma((ranks, width // wide)),
            dma((ranks, width // wide)), dma((ranks, width // wide)),
            dma((ranks, blocks)), dma((ranks, blocks)),
            dma((ranks, blocks)), dma((ranks, blocks)),
        ],
        compiler_params=pltpu.CompilerParams(
            collective_id=0, has_side_effects=True, vmem_limit_bytes=32 * 2**20
        ),
    )(keep(acts), keep(hidden_grad), keep(counts), keep(momentum), keep(act_grad))
    new_momentum, gram, received = pl.pallas_call(
        functools.partial(write_out, (4, 2, 2)),
        out_shape=tuple(pltpu.HBM(r.shape, r.dtype) for r in results),
        in_specs=[in_vmem] * 3,
        out_specs=(hbm,) * 3,
        scratch_shapes=[dma((8,))],
    )(*[pltpu.with_memory_space_constraint(r, vmem) for r in results])
    return (new_momentum[None, None], gram[None, None], received)


def solution(mesh):
    return jax.shard_map(
        on_device,
        mesh=mesh,
        in_specs=(
            P("pipe", "expert", None, None),
            P("pipe", None, None, "tensor"),
            P("pipe", None, None),
            P("pipe", "expert", "tensor", None),
            P("pipe", "expert", "tensor"),
        ),
        out_specs=(
            P("pipe", "expert", "tensor", None),
            P("pipe", "expert", "tensor", None),
            P("pipe", "expert", "tensor"),
        ),
        check_vma=False,
    )
```

```python
import functools

import jax
import jax.numpy as jnp
from jax import lax
from jax.experimental import pallas as pl
from jax.experimental.pallas import tpu as pltpu
from jax.sharding import PartitionSpec as P

D = 3584
PANEL = 512
DECAY = 0.9
MESH = pl.DeviceIdType.MESH


def kernel(
    sections, ranks,
    acts, hidden, counts_in, momentum, act_grad,
    new_momentum, gram, received,
    counts, x_buf, g_own, m_buf, xt_buf, g_in, nt_buf, own, send1, recv1, send2, recv2,
    load_sem, shift_send, shift_recv,
    d_send, d_recv, g_send, g_recv, f_send, f_recv, s1_send, s1_recv, s2_send, s2_recv,
):
    section = lax.axis_index("pipe")
    expert_rank = lax.axis_index("expert")
    rank = lax.axis_index("tensor")
    pair = expert_rank // 2
    half = expert_rank % 2
    other_half = expert_rank + 1 - 2 * half
    partner = {"expert": other_half}
    row_count, features = x_buf.shape
    rows, hidden_units = new_momentum.shape
    q, wide = send1.shape[2:]
    per_rank = g_own.shape[1] // wide
    share = row_count // 2
    subs = 2 if q % 128 == 0 else 1
    thin = wide // subs
    first, last = section == 0, section == sections - 1

    if features == rows:
        x_src = acts.at[0, 0, :, pl.ds(pl.multiple_of(rank * rows, 128), rows)]
    else:
        x_src = acts.at[0, 0]
    load_x = pltpu.make_async_copy(x_src, x_buf, load_sem.at[0])
    load_g = pltpu.make_async_copy(hidden.at[0, pair], g_own, load_sem.at[1])
    load_m = pltpu.make_async_copy(momentum.at[0, 0], m_buf, load_sem.at[2])
    load_counts = pltpu.make_async_copy(counts_in, counts, load_sem.at[3])
    load_g.start()

    barrier = pltpu.get_barrier_semaphore()
    pl.semaphore_signal(barrier, inc=1, device_id=partner, device_id_type=MESH)
    for k in range(1, ranks):
        pl.semaphore_signal(
            barrier, inc=1, device_id={"tensor": (rank + k) % ranks}, device_id_type=MESH
        )
        pl.semaphore_signal(
            barrier,
            inc=1,
            device_id={"expert": other_half, "tensor": (rank + k) % ranks},
            device_id_type=MESH,
        )

    @pl.when(jnp.logical_not(first))
    def _():
        pl.semaphore_signal(barrier, inc=1, device_id={"pipe": section - 1}, device_id_type=MESH)

    @pl.when(jnp.logical_not(last))
    def _():
        pl.semaphore_signal(barrier, inc=1, device_id={"pipe": section + 1}, device_id_type=MESH)

    ends = jnp.where(first, 1, 0) + jnp.where(last, 1, 0)
    load_x.start()
    load_counts.start()
    load_m.start()
    load_g.wait()
    pl.semaphore_wait(barrier, 2 * ranks + 1 - ends)

    shift = pltpu.make_async_remote_copy(
        src_ref=act_grad,
        dst_ref=received,
        send_sem=shift_send,
        recv_sem=shift_recv,
        device_id={"pipe": section - 1},
        device_id_type=MESH,
    )

    def clear_dead_rows():
        row = lax.broadcasted_iota(jnp.int32, (row_count, 1), 0)
        micro = counts.shape[2]
        block = row_count // micro
        limit = jnp.zeros((row_count, 1), jnp.int32)
        for b in range(micro):
            inside = jnp.logical_and(row >= b * block, row < (b + 1) * block)
            limit = jnp.where(inside, counts[0, pair, b] + b * block, limit)
        live = jnp.where(row < limit, 1.0, 0.0).astype(jnp.float32)
        masked = (x_buf[...].astype(jnp.float32) * live).astype(jnp.bfloat16)
        xt_buf[...] = masked.T

    def own_share(which):
        return pl.ds(pl.multiple_of(which * share, share), share)

    def as_rank(me):
        peers = [(me + k) % ranks for k in range(1, ranks)]

        def send_share(peer, c):
            return pltpu.make_async_remote_copy(
                src_ref=g_own.at[own_share(half), pl.ds(c * wide, wide)],
                dst_ref=g_in.at[me, c, own_share(half)],
                send_sem=g_send.at[peer, c],
                recv_sem=g_recv.at[me, c],
                device_id={"tensor": peer},
                device_id_type=MESH,
            )

        def arrived_share(peer, c):
            place = g_in.at[peer, c, own_share(half)]
            return pltpu.make_async_remote_copy(
                src_ref=place,
                dst_ref=place,
                send_sem=g_send.at[peer, c],
                recv_sem=g_recv.at[peer, c],
                device_id={"tensor": peer},
                device_id_type=MESH,
            )

        def forward(peer, c, which):
            place = g_in.at[peer, c, own_share(which)]
            return pltpu.make_async_remote_copy(
                src_ref=place,
                dst_ref=place,
                send_sem=f_send.at[peer, c],
                recv_sem=f_recv.at[peer, c],
                device_id=partner,
                device_id_type=MESH,
            )

        def direct(peer, c):
            return c == 0 and peer * per_rank < ranks

        def send_direct(peer, away, sub):
            target = {"tensor": peer}
            if away:
                target["expert"] = other_half
            cols = pl.ds(sub * thin, thin)
            return pltpu.make_async_remote_copy(
                src_ref=g_own.at[own_share(half), cols],
                dst_ref=g_in.at[me, 0, own_share(half), cols],
                send_sem=d_send.at[peer, away, sub],
                recv_sem=d_recv.at[me, away, sub],
                device_id=target,
                device_id_type=MESH,
            )

        def arrived_direct(peer, away, sub):
            which = 1 - half if away else half
            place = g_in.at[peer, 0, own_share(which), pl.ds(sub * thin, thin)]
            return pltpu.make_async_remote_copy(
                src_ref=place,
                dst_ref=place,
                send_sem=d_send.at[peer, away, sub],
                recv_sem=d_recv.at[peer, away, sub],
                device_id={"tensor": peer},
                device_id_type=MESH,
            )

        def to_partner(owner, j):
            return pltpu.make_async_remote_copy(
                src_ref=send1.at[owner, j],
                dst_ref=recv1.at[owner, j],
                send_sem=s1_send.at[owner, j],
                recv_sem=s1_recv.at[owner, j],
                device_id=partner,
                device_id_type=MESH,
            )

        def to_rank(peer, slot, j):
            return pltpu.make_async_remote_copy(
                src_ref=send2.at[peer, j],
                dst_ref=recv2.at[slot, j],
                send_sem=s2_send.at[peer, j],
                recv_sem=s2_recv.at[slot, j],
                device_id={"tensor": peer},
                device_id_type=MESH,
            )

        for c in range(per_rank):
            if direct(me, c):
                for sub in range(subs):
                    for peer in peers:
                        for away in range(2):
                            send_direct(peer, away, sub).start()
            else:
                for peer in peers:
                    send_share(peer, c).start()

        @pl.when(jnp.logical_not(first))
        def _():
            shift.start()

        load_x.wait()
        load_counts.wait()
        clear_dead_rows()
        load_m.wait()

        flipped = set()

        def update(j, gradients, at=0):
            size = gradients.shape[1]
            cols = pl.ds(j * wide + at, size)
            if features == rows:
                x_rows = xt_buf[...]
            else:
                x_rows = xt_buf[pl.ds(me * rows, rows), :]
            grad = jnp.dot(x_rows, gradients, preferred_element_type=jnp.float32)
            grad = grad.astype(jnp.bfloat16).astype(jnp.float32)
            new = (DECAY * m_buf[:, cols].astype(jnp.float32) + grad).astype(jnp.bfloat16)
            new_momentum[:, cols] = new
            if at or size < wide:
                nt_buf[j, pl.ds(at, size)] = new.T
                flipped.add(j)

        def piece(owner, j):
            if owner not in flipped:
                nt_buf[owner] = new_momentum[:, pl.ds(owner * wide, wide)].T
                flipped.add(owner)
            sums = jnp.dot(
                nt_buf[owner],
                new_momentum[:, pl.ds(j * wide, wide)],
                preferred_element_type=jnp.float32,
            )
            top, bottom = sums[:q], sums[q:]
            own[owner, j] = jnp.where(half == 0, top, bottom)
            send1[owner, j] = jnp.where(half == 0, bottom, top).astype(jnp.bfloat16)
            to_partner(owner, j).start()

        def half_piece(owner, j, keeper):
            sums = jnp.dot(
                nt_buf[owner, pl.ds(keeper * q, q)],
                new_momentum[:, pl.ds(j * wide, wide)],
                preferred_element_type=jnp.float32,
            )

            @pl.when(half == keeper)
            def _():
                own[owner, j] = sums

            @pl.when(half != keeper)
            def _():
                send1[owner, j] = sums.astype(jnp.bfloat16)
                to_partner(owner, j).start()

        def pass_on(owner, j):
            to_partner(owner, j).wait_recv()
            both = own[owner, j] + recv1[owner, j].astype(jnp.float32)
            send2[owner, j] = both.astype(jnp.bfloat16)
            to_rank(owner, me, j).start()

        arrivals = [(peer, c) for c in range(per_rank) for peer in peers]
        coming = [a for a in arrivals if not direct(*a)]

        def forward_next():
            if coming:
                peer, c = coming.pop(0)
                arrived_share(peer, c).wait_recv()
                forward(peer, c, half).start()

        ready, waiting = [], []

        def pieces(new, forward_after, done=()):
            ready.extend(new)
            todo = [
                (owner, j)
                for owner in peers + [me]
                if owner in ready
                for j in (ready if owner in new else new)
                if (owner, j) not in done
            ]
            for n, (owner, j) in enumerate(todo):
                piece(owner, j)
                if n in forward_after:
                    forward_next()
                waiting[:] = [(owner, j, age + 1) for owner, j, age in waiting]
                while waiting and waiting[0][2] >= 2:
                    pass_on(*waiting.pop(0)[:2])
                if owner != me:
                    waiting.append((owner, j, 0))

        mine = [me * per_rank + c for c in range(per_rank)]
        for c in range(per_rank):
            update(mine[c], g_own[:, c * wide:(c + 1) * wide])
        pieces(mine, (1, 3))

        @pl.when(last)
        def _():
            received[...] = jnp.zeros_like(received)

        for peer, c in arrivals:
            j = peer * per_rank + c
            if direct(peer, c):
                before = list(ready)
                for sub in range(subs):
                    for away in range(2):
                        arrived_direct(peer, away, sub).wait_recv()
                    update(j, g_in[peer, c, :, pl.ds(sub * thin, thin)], sub * thin)
                    if subs == 2:
                        for i in before:
                            half_piece(j, i, sub)
                done = [(j, i) for i in before] if subs == 2 else []
                if done and j != me:

                    @pl.when(half == 0)
                    def _():
                        for item in done:
                            pass_on(*item)

                pieces([j], (0,), done)
                if done and j != me:

                    @pl.when(half == 1)
                    def _():
                        for item in done:
                            pass_on(*item)

                continue
            if (peer, c) in coming:
                forward_next()
            while waiting:
                pass_on(*waiting.pop(0)[:2])
            forward(peer, c, 1 - half).wait_recv()
            update(j, g_in[peer, c])
            pieces([j], (0,))
        while waiting:
            pass_on(*waiting.pop(0)[:2])

        order = ready
        for j in order:
            to_partner(me, j).wait_recv()
            own[me, j] = own[me, j] + recv1[me, j].astype(jnp.float32)
        for j in order[per_rank:] + order[:per_rank]:
            total = own[me, j]
            for peer in peers:
                to_rank(peer, peer, j).wait_recv()
                total = total + recv2[peer, j].astype(jnp.float32)
            gram[:, pl.ds(j * wide, wide)] = total / D

        for peer, c in arrivals:
            if direct(me, c):
                for sub in range(subs):
                    for away in range(2):
                        send_direct(peer, away, sub).wait_send()
            else:
                send_share(peer, c).wait_send()
            if not direct(peer, c):
                forward(peer, c, half).wait_send()
        for j in order:
            for owner in peers + [me]:
                to_partner(owner, j).wait_send()
            for peer in peers:
                to_rank(peer, me, j).wait_send()

    for me in range(ranks):

        @pl.when(rank == me)
        def _():
            as_rank(me)

    @pl.when(jnp.logical_not(first))
    def _():
        shift.wait_send()

    @pl.when(jnp.logical_not(last))
    def _():
        shift.wait_recv()


def write_out(cuts, *refs):
    count = len(cuts)
    sems = refs[-1]
    copies = []
    for i, cut in enumerate(cuts):
        rows = refs[i].shape[-2] // cut
        for n in range(cut):
            place = (slice(None),) * (len(refs[i].shape) - 2) + (pl.ds(n * rows, rows),)
            copies.append(
                pltpu.make_async_copy(
                    refs[i].at[place], refs[count + i].at[place], sems.at[len(copies)]
                )
            )
    for copy in copies:
        copy.start()
    for copy in copies:
        copy.wait()


def on_device(acts, hidden_grad, counts, momentum, act_grad):
    sections, ranks = lax.axis_size("pipe"), lax.axis_size("tensor")
    row_count, features = acts.shape[2:]
    rows, units = momentum.shape[2:]
    width = hidden_grad.shape[3]
    q = PANEL // (2 * ranks)
    wide = 2 * q
    blocks = units // wide
    x_cols = rows if rows % 128 == 0 else features
    bf16, f32 = jnp.bfloat16, jnp.float32
    vmem, dma = pltpu.VMEM, pltpu.SemaphoreType.DMA
    hbm = pl.BlockSpec(memory_space=pltpu.HBM)
    anywhere = pl.BlockSpec(memory_space=pl.ANY)
    in_vmem = pl.BlockSpec(memory_space=vmem)

    def keep(x):
        return pltpu.with_memory_space_constraint(x, pltpu.HBM)

    results = pl.pallas_call(
        functools.partial(kernel, sections, ranks),
        out_shape=(
            vmem((rows, units), bf16),
            vmem((q, units), f32),
            vmem(act_grad.shape, bf16),
        ),
        in_specs=[hbm] * 5,
        out_specs=(in_vmem, in_vmem, in_vmem),
        scratch_shapes=[
            pltpu.SMEM(counts.shape, counts.dtype),
            vmem((row_count, x_cols), bf16),
            vmem((row_count, width), bf16),
            vmem((rows, units), bf16),
            vmem((x_cols, row_count), bf16),
            vmem((ranks, width // wide, row_count, wide), bf16),
            vmem((ranks, wide, rows), bf16),
            vmem((ranks, blocks, q, wide), f32),
            vmem((ranks, blocks, q, wide), bf16),
            vmem((ranks, blocks, q, wide), bf16),
            vmem((ranks, blocks, q, wide), bf16),
            vmem((ranks, blocks, q, wide), bf16),
            dma((4,)), dma, dma,
            dma((ranks, 2, 2)), dma((ranks, 2, 2)),
            dma((ranks, width // wide)), dma((ranks, width // wide)),
            dma((ranks, width // wide)), dma((ranks, width // wide)),
            dma((ranks, blocks)), dma((ranks, blocks)),
            dma((ranks, blocks)), dma((ranks, blocks)),
        ],
        compiler_params=pltpu.CompilerParams(
            collective_id=0, has_side_effects=True, vmem_limit_bytes=32 * 2**20
        ),
    )(keep(acts), keep(hidden_grad), keep(counts), keep(momentum), keep(act_grad))
    new_momentum, gram, received = pl.pallas_call(
        functools.partial(write_out, (4, 2, 2)),
        out_shape=tuple(pltpu.HBM(r.shape, r.dtype) for r in results),
        in_specs=[in_vmem] * 3,
        out_specs=(hbm,) * 3,
        scratch_shapes=[dma((8,))],
    )(*[pltpu.with_memory_space_constraint(r, vmem) for r in results])
    return (new_momentum[None, None], gram[None, None], received)


def solution(mesh):
    return jax.shard_map(
        on_device,
        mesh=mesh,
        in_specs=(
            P("pipe", "expert", None, None),
            P("pipe", None, None, "tensor"),
            P("pipe", None, None),
            P("pipe", "expert", "tensor", None),
            P("pipe", "expert", "tensor"),
        ),
        out_specs=(
            P("pipe", "expert", "tensor", None),
            P("pipe", "expert", "tensor", None),
            P("pipe", "expert", "tensor"),
        ),
        check_vma=False,
    )
```

```python
import functools

import jax
import jax.numpy as jnp
from jax import lax
from jax.experimental import pallas as pl
from jax.experimental.pallas import tpu as pltpu
from jax.sharding import PartitionSpec as P

D = 3584
PANEL = 512
DECAY = 0.9
MESH = pl.DeviceIdType.MESH


def kernel(
    sections, ranks,
    acts, hidden, counts_in, momentum, act_grad,
    new_momentum, gram, received,
    counts, x_buf, g_own, m_buf, xt_buf, g_in, nt_buf, own, send1, recv1, send2, recv2,
    load_sem, shift_send, shift_recv,
    g_send, g_recv, f_send, f_recv, s1_send, s1_recv, s2_send, s2_recv,
):
    section = lax.axis_index("pipe")
    expert_rank = lax.axis_index("expert")
    rank = lax.axis_index("tensor")
    pair = expert_rank // 2
    half = expert_rank % 2
    partner = {"expert": expert_rank + 1 - 2 * half}
    row_count, features = x_buf.shape
    rows, hidden_units = new_momentum.shape
    q, wide = send1.shape[2:]
    per_rank = g_own.shape[1] // wide
    share = row_count // 2
    first, last = section == 0, section == sections - 1

    if features == rows:
        x_src = acts.at[0, 0, :, pl.ds(pl.multiple_of(rank * rows, 128), rows)]
    else:
        x_src = acts.at[0, 0]
    load_x = pltpu.make_async_copy(x_src, x_buf, load_sem.at[0])
    load_g = pltpu.make_async_copy(hidden.at[0, pair], g_own, load_sem.at[1])
    load_m = pltpu.make_async_copy(momentum.at[0, 0], m_buf, load_sem.at[2])
    load_counts = pltpu.make_async_copy(counts_in, counts, load_sem.at[3])
    load_g.start()

    barrier = pltpu.get_barrier_semaphore()
    pl.semaphore_signal(barrier, inc=1, device_id=partner, device_id_type=MESH)
    for k in range(1, ranks):
        pl.semaphore_signal(
            barrier, inc=1, device_id={"tensor": (rank + k) % ranks}, device_id_type=MESH
        )

    @pl.when(jnp.logical_not(first))
    def _():
        pl.semaphore_signal(barrier, inc=1, device_id={"pipe": section - 1}, device_id_type=MESH)

    @pl.when(jnp.logical_not(last))
    def _():
        pl.semaphore_signal(barrier, inc=1, device_id={"pipe": section + 1}, device_id_type=MESH)

    ends = jnp.where(first, 1, 0) + jnp.where(last, 1, 0)
    load_x.start()
    load_counts.start()
    load_m.start()
    load_g.wait()
    pl.semaphore_wait(barrier, ranks + 2 - ends)

    shift = pltpu.make_async_remote_copy(
        src_ref=act_grad,
        dst_ref=received,
        send_sem=shift_send,
        recv_sem=shift_recv,
        device_id={"pipe": section - 1},
        device_id_type=MESH,
    )

    def clear_dead_rows():
        row = lax.broadcasted_iota(jnp.int32, (row_count, 1), 0)
        micro = counts.shape[2]
        block = row_count // micro
        limit = jnp.zeros((row_count, 1), jnp.int32)
        for b in range(micro):
            inside = jnp.logical_and(row >= b * block, row < (b + 1) * block)
            limit = jnp.where(inside, counts[0, pair, b] + b * block, limit)
        live = jnp.where(row < limit, 1.0, 0.0).astype(jnp.float32)
        masked = (x_buf[...].astype(jnp.float32) * live).astype(jnp.bfloat16)
        xt_buf[...] = masked.T

    def own_share(which):
        return pl.ds(pl.multiple_of(which * share, share), share)

    def as_rank(me):
        peers = [(me + k) % ranks for k in range(1, ranks)]

        def send_share(peer, c):
            return pltpu.make_async_remote_copy(
                src_ref=g_own.at[own_share(half), pl.ds(c * wide, wide)],
                dst_ref=g_in.at[me, c, own_share(half)],
                send_sem=g_send.at[peer, c],
                recv_sem=g_recv.at[me, c],
                device_id={"tensor": peer},
                device_id_type=MESH,
            )

        def arrived_share(peer, c):
            place = g_in.at[peer, c, own_share(half)]
            return pltpu.make_async_remote_copy(
                src_ref=place,
                dst_ref=place,
                send_sem=g_send.at[peer, c],
                recv_sem=g_recv.at[peer, c],
                device_id={"tensor": peer},
                device_id_type=MESH,
            )

        def forward(peer, c, which):
            place = g_in.at[peer, c, own_share(which)]
            return pltpu.make_async_remote_copy(
                src_ref=place,
                dst_ref=place,
                send_sem=f_send.at[peer, c],
                recv_sem=f_recv.at[peer, c],
                device_id=partner,
                device_id_type=MESH,
            )

        def to_partner(owner, j):
            return pltpu.make_async_remote_copy(
                src_ref=send1.at[owner, j],
                dst_ref=recv1.at[owner, j],
                send_sem=s1_send.at[owner, j],
                recv_sem=s1_recv.at[owner, j],
                device_id=partner,
                device_id_type=MESH,
            )

        def to_rank(peer, slot, j):
            return pltpu.make_async_remote_copy(
                src_ref=send2.at[peer, j],
                dst_ref=recv2.at[slot, j],
                send_sem=s2_send.at[peer, j],
                recv_sem=s2_recv.at[slot, j],
                device_id={"tensor": peer},
                device_id_type=MESH,
            )

        for c in range(per_rank):
            for peer in peers:
                send_share(peer, c).start()

        @pl.when(jnp.logical_not(first))
        def _():
            shift.start()

        load_x.wait()
        load_counts.wait()
        clear_dead_rows()
        load_m.wait()

        flipped = set()

        def update(j, gradients):
            cols = pl.ds(j * wide, wide)
            if features == rows:
                x_rows = xt_buf[...]
            else:
                x_rows = xt_buf[pl.ds(me * rows, rows), :]
            grad = jnp.dot(x_rows, gradients, preferred_element_type=jnp.float32)
            grad = grad.astype(jnp.bfloat16).astype(jnp.float32)
            new = (DECAY * m_buf[:, cols].astype(jnp.float32) + grad).astype(jnp.bfloat16)
            new_momentum[:, cols] = new

        def piece(owner, j):
            if owner not in flipped:
                nt_buf[owner] = new_momentum[:, pl.ds(owner * wide, wide)].T
                flipped.add(owner)
            sums = jnp.dot(
                nt_buf[owner],
                new_momentum[:, pl.ds(j * wide, wide)],
                preferred_element_type=jnp.float32,
            )
            top, bottom = sums[:q], sums[q:]
            own[owner, j] = jnp.where(half == 0, top, bottom)
            send1[owner, j] = jnp.where(half == 0, bottom, top).astype(jnp.bfloat16)
            to_partner(owner, j).start()

        def pass_on(owner, j):
            to_partner(owner, j).wait_recv()
            both = own[owner, j] + recv1[owner, j].astype(jnp.float32)
            send2[owner, j] = both.astype(jnp.bfloat16)
            to_rank(owner, me, j).start()

        arrivals = [(peer, c) for c in range(per_rank) for peer in peers]
        coming = list(arrivals)

        def forward_next():
            if coming:
                peer, c = coming.pop(0)
                arrived_share(peer, c).wait_recv()
                forward(peer, c, half).start()

        ready, waiting = [], []

        def pieces(new, forward_after=()):
            ready.extend(new)
            todo = [
                (owner, j)
                for owner in peers + [me]
                if owner in ready
                for j in (ready if owner in new else new)
            ]
            for n, (owner, j) in enumerate(todo):
                piece(owner, j)
                if n in forward_after:
                    forward_next()
                waiting[:] = [(owner, j, age + 1) for owner, j, age in waiting]
                while waiting and (waiting[0][2] >= 2 or n == 0):
                    pass_on(*waiting.pop(0)[:2])
                if owner != me:
                    waiting.append((owner, j, 0))

        mine = [me * per_rank + c for c in range(per_rank)]
        for c in range(per_rank):
            update(mine[c], g_own[:, c * wide:(c + 1) * wide])
            if c == 0:
                forward_next()
        pieces(mine, (1,))

        @pl.when(last)
        def _():
            received[...] = jnp.zeros_like(received)

        for peer, c in arrivals:
            j = peer * per_rank + c
            if (peer, c) in coming:
                forward_next()
            forward(peer, c, 1 - half).wait_recv()
            forward_next()
            update(j, g_in[peer, c])
            pieces([j])
        while waiting:
            pass_on(*waiting.pop(0)[:2])

        order = ready
        for j in order:
            to_partner(me, j).wait_recv()
            own[me, j] = own[me, j] + recv1[me, j].astype(jnp.float32)
        for j in order[per_rank:] + order[:per_rank]:
            total = own[me, j]
            for peer in peers:
                to_rank(peer, peer, j).wait_recv()
                total = total + recv2[peer, j].astype(jnp.float32)
            gram[:, pl.ds(j * wide, wide)] = total / D

        for peer, c in arrivals:
            send_share(peer, c).wait_send()
            forward(peer, c, half).wait_send()
        for j in order:
            for owner in peers + [me]:
                to_partner(owner, j).wait_send()
            for peer in peers:
                to_rank(peer, me, j).wait_send()

    for me in range(ranks):

        @pl.when(rank == me)
        def _():
            as_rank(me)

    @pl.when(jnp.logical_not(first))
    def _():
        shift.wait_send()

    @pl.when(jnp.logical_not(last))
    def _():
        shift.wait_recv()


def write_out(cuts, *refs):
    count = len(cuts)
    sems = refs[-1]
    copies = []
    for i, cut in enumerate(cuts):
        rows = refs[i].shape[-2] // cut
        for n in range(cut):
            place = (slice(None),) * (len(refs[i].shape) - 2) + (pl.ds(n * rows, rows),)
            copies.append(
                pltpu.make_async_copy(
                    refs[i].at[place], refs[count + i].at[place], sems.at[len(copies)]
                )
            )
    for copy in copies:
        copy.start()
    for copy in copies:
        copy.wait()


def on_device(acts, hidden_grad, counts, momentum, act_grad):
    sections, ranks = lax.axis_size("pipe"), lax.axis_size("tensor")
    row_count, features = acts.shape[2:]
    rows, units = momentum.shape[2:]
    width = hidden_grad.shape[3]
    q = PANEL // (2 * ranks)
    wide = 2 * q
    blocks = units // wide
    x_cols = rows if rows % 128 == 0 else features
    bf16, f32 = jnp.bfloat16, jnp.float32
    vmem, dma = pltpu.VMEM, pltpu.SemaphoreType.DMA
    hbm = pl.BlockSpec(memory_space=pltpu.HBM)
    anywhere = pl.BlockSpec(memory_space=pl.ANY)
    in_vmem = pl.BlockSpec(memory_space=vmem)

    def keep(x):
        return pltpu.with_memory_space_constraint(x, pltpu.HBM)

    results = pl.pallas_call(
        functools.partial(kernel, sections, ranks),
        out_shape=(
            vmem((rows, units), bf16),
            vmem((q, units), f32),
            vmem(act_grad.shape, bf16),
        ),
        in_specs=[hbm] * 5,
        out_specs=(in_vmem, in_vmem, in_vmem),
        scratch_shapes=[
            pltpu.SMEM(counts.shape, counts.dtype),
            vmem((row_count, x_cols), bf16),
            vmem((row_count, width), bf16),
            vmem((rows, units), bf16),
            vmem((x_cols, row_count), bf16),
            vmem((ranks, width // wide, row_count, wide), bf16),
            vmem((ranks, wide, rows), bf16),
            vmem((ranks, blocks, q, wide), f32),
            vmem((ranks, blocks, q, wide), bf16),
            vmem((ranks, blocks, q, wide), bf16),
            vmem((ranks, blocks, q, wide), bf16),
            vmem((ranks, blocks, q, wide), bf16),
            dma((4,)), dma, dma,
            dma((ranks, width // wide)), dma((ranks, width // wide)),
            dma((ranks, width // wide)), dma((ranks, width // wide)),
            dma((ranks, blocks)), dma((ranks, blocks)),
            dma((ranks, blocks)), dma((ranks, blocks)),
        ],
        compiler_params=pltpu.CompilerParams(
            collective_id=0, has_side_effects=True, vmem_limit_bytes=32 * 2**20
        ),
    )(keep(acts), keep(hidden_grad), keep(counts), keep(momentum), keep(act_grad))
    new_momentum, gram, received = pl.pallas_call(
        functools.partial(write_out, (4, 2, 2)),
        out_shape=tuple(pltpu.HBM(r.shape, r.dtype) for r in results),
        in_specs=[in_vmem] * 3,
        out_specs=(hbm,) * 3,
        scratch_shapes=[dma((8,))],
    )(*[pltpu.with_memory_space_constraint(r, vmem) for r in results])
    return (new_momentum[None, None], gram[None, None], received)


def solution(mesh):
    return jax.shard_map(
        on_device,
        mesh=mesh,
        in_specs=(
            P("pipe", "expert", None, None),
            P("pipe", None, None, "tensor"),
            P("pipe", None, None),
            P("pipe", "expert", "tensor", None),
            P("pipe", "expert", "tensor"),
        ),
        out_specs=(
            P("pipe", "expert", "tensor", None),
            P("pipe", "expert", "tensor", None),
            P("pipe", "expert", "tensor"),
        ),
        check_vma=False,
    )
```

```python
import functools

import jax
import jax.numpy as jnp
from jax import lax
from jax.experimental import pallas as pl
from jax.experimental.pallas import tpu as pltpu
from jax.sharding import PartitionSpec as P

D = 3584
PANEL = 512
DECAY = 0.9
MESH = pl.DeviceIdType.MESH


def kernel(
    sections, ranks,
    acts, hidden, counts_in, momentum, act_grad,
    new_momentum, gram, received,
    counts, x_buf, g_own, m_buf, xt_buf, g_in, nt_buf, own, send1, recv1, send2, recv2,
    load_sem, shift_send, shift_recv,
    d_send, d_recv, g_send, g_recv, f_send, f_recv, s1_send, s1_recv, s2_send, s2_recv,
):
    section = lax.axis_index("pipe")
    expert_rank = lax.axis_index("expert")
    rank = lax.axis_index("tensor")
    pair = expert_rank // 2
    half = expert_rank % 2
    other_half = expert_rank + 1 - 2 * half
    partner = {"expert": other_half}
    row_count, features = x_buf.shape
    rows, hidden_units = new_momentum.shape
    q, wide = send1.shape[2:]
    per_rank = g_own.shape[1] // wide
    share = row_count // 2
    subs = 2 if q % 128 == 0 else 1
    thin = wide // subs
    first, last = section == 0, section == sections - 1

    if features == rows:
        x_src = acts.at[0, 0, :, pl.ds(pl.multiple_of(rank * rows, 128), rows)]
    else:
        x_src = acts.at[0, 0]
    load_x = pltpu.make_async_copy(x_src, x_buf, load_sem.at[0])
    load_g = pltpu.make_async_copy(hidden.at[0, pair], g_own, load_sem.at[1])
    load_m = pltpu.make_async_copy(momentum.at[0, 0], m_buf, load_sem.at[2])
    load_counts = pltpu.make_async_copy(counts_in, counts, load_sem.at[3])
    load_g.start()

    barrier = pltpu.get_barrier_semaphore()
    pl.semaphore_signal(barrier, inc=1, device_id=partner, device_id_type=MESH)
    for k in range(1, ranks):
        pl.semaphore_signal(
            barrier, inc=1, device_id={"tensor": (rank + k) % ranks}, device_id_type=MESH
        )
        pl.semaphore_signal(
            barrier,
            inc=1,
            device_id={"expert": other_half, "tensor": (rank + k) % ranks},
            device_id_type=MESH,
        )

    @pl.when(jnp.logical_not(first))
    def _():
        pl.semaphore_signal(barrier, inc=1, device_id={"pipe": section - 1}, device_id_type=MESH)

    @pl.when(jnp.logical_not(last))
    def _():
        pl.semaphore_signal(barrier, inc=1, device_id={"pipe": section + 1}, device_id_type=MESH)

    ends = jnp.where(first, 1, 0) + jnp.where(last, 1, 0)
    load_x.start()
    load_counts.start()
    load_m.start()
    load_g.wait()
    pl.semaphore_wait(barrier, 2 * ranks + 1 - ends)

    shift = pltpu.make_async_remote_copy(
        src_ref=act_grad,
        dst_ref=received,
        send_sem=shift_send,
        recv_sem=shift_recv,
        device_id={"pipe": section - 1},
        device_id_type=MESH,
    )

    def clear_dead_rows():
        row = lax.broadcasted_iota(jnp.int32, (row_count, 1), 0)
        micro = counts.shape[2]
        block = row_count // micro
        limit = jnp.zeros((row_count, 1), jnp.int32)
        for b in range(micro):
            inside = jnp.logical_and(row >= b * block, row < (b + 1) * block)
            limit = jnp.where(inside, counts[0, pair, b] + b * block, limit)
        live = jnp.where(row < limit, 1.0, 0.0).astype(jnp.float32)
        masked = (x_buf[...].astype(jnp.float32) * live).astype(jnp.bfloat16)
        xt_buf[...] = masked.T

    def own_share(which):
        return pl.ds(pl.multiple_of(which * share, share), share)

    def as_rank(me):
        peers = [(me + k) % ranks for k in range(1, ranks)]

        def send_share(peer, c):
            return pltpu.make_async_remote_copy(
                src_ref=g_own.at[own_share(half), pl.ds(c * wide, wide)],
                dst_ref=g_in.at[me, c, own_share(half)],
                send_sem=g_send.at[peer, c],
                recv_sem=g_recv.at[me, c],
                device_id={"tensor": peer},
                device_id_type=MESH,
            )

        def arrived_share(peer, c):
            place = g_in.at[peer, c, own_share(half)]
            return pltpu.make_async_remote_copy(
                src_ref=place,
                dst_ref=place,
                send_sem=g_send.at[peer, c],
                recv_sem=g_recv.at[peer, c],
                device_id={"tensor": peer},
                device_id_type=MESH,
            )

        def forward(peer, c, which):
            place = g_in.at[peer, c, own_share(which)]
            return pltpu.make_async_remote_copy(
                src_ref=place,
                dst_ref=place,
                send_sem=f_send.at[peer, c],
                recv_sem=f_recv.at[peer, c],
                device_id=partner,
                device_id_type=MESH,
            )

        def direct(peer, c):
            return c == 0 and peer * per_rank < ranks

        def send_direct(peer, away, sub):
            target = {"tensor": peer}
            if away:
                target["expert"] = other_half
            cols = pl.ds(sub * thin, thin)
            return pltpu.make_async_remote_copy(
                src_ref=g_own.at[own_share(half), cols],
                dst_ref=g_in.at[me, 0, own_share(half), cols],
                send_sem=d_send.at[peer, away, sub],
                recv_sem=d_recv.at[me, away, sub],
                device_id=target,
                device_id_type=MESH,
            )

        def arrived_direct(peer, away, sub):
            which = 1 - half if away else half
            place = g_in.at[peer, 0, own_share(which), pl.ds(sub * thin, thin)]
            return pltpu.make_async_remote_copy(
                src_ref=place,
                dst_ref=place,
                send_sem=d_send.at[peer, away, sub],
                recv_sem=d_recv.at[peer, away, sub],
                device_id={"tensor": peer},
                device_id_type=MESH,
            )

        def to_partner(owner, j):
            return pltpu.make_async_remote_copy(
                src_ref=send1.at[owner, j],
                dst_ref=recv1.at[owner, j],
                send_sem=s1_send.at[owner, j],
                recv_sem=s1_recv.at[owner, j],
                device_id=partner,
                device_id_type=MESH,
            )

        def to_rank(peer, slot, j):
            return pltpu.make_async_remote_copy(
                src_ref=send2.at[peer, j],
                dst_ref=recv2.at[slot, j],
                send_sem=s2_send.at[peer, j],
                recv_sem=s2_recv.at[slot, j],
                device_id={"tensor": peer},
                device_id_type=MESH,
            )

        for c in range(per_rank):
            if direct(me, c):
                for sub in range(subs):
                    for peer in peers:
                        for away in range(2):
                            send_direct(peer, away, sub).start()
            else:
                for peer in peers:
                    send_share(peer, c).start()

        @pl.when(jnp.logical_not(first))
        def _():
            shift.start()

        load_x.wait()
        load_counts.wait()
        clear_dead_rows()
        load_m.wait()

        flipped = set()

        def update(j, gradients, at=0):
            size = gradients.shape[1]
            cols = pl.ds(j * wide + at, size)
            if features == rows:
                x_rows = xt_buf[...]
            else:
                x_rows = xt_buf[pl.ds(me * rows, rows), :]
            grad = jnp.dot(x_rows, gradients, preferred_element_type=jnp.float32)
            grad = grad.astype(jnp.bfloat16).astype(jnp.float32)
            new = (DECAY * m_buf[:, cols].astype(jnp.float32) + grad).astype(jnp.bfloat16)
            new_momentum[:, cols] = new
            if at or size < wide:
                nt_buf[j, pl.ds(at, size)] = new.T
                flipped.add(j)

        def piece(owner, j):
            if owner not in flipped:
                nt_buf[owner] = new_momentum[:, pl.ds(owner * wide, wide)].T
                flipped.add(owner)
            sums = jnp.dot(
                nt_buf[owner],
                new_momentum[:, pl.ds(j * wide, wide)],
                preferred_element_type=jnp.float32,
            )
            top, bottom = sums[:q], sums[q:]
            own[owner, j] = jnp.where(half == 0, top, bottom)
            send1[owner, j] = jnp.where(half == 0, bottom, top).astype(jnp.bfloat16)
            to_partner(owner, j).start()

        def half_pieces(owner, start, count, keeper):
            sums = jnp.dot(
                nt_buf[owner, pl.ds(keeper * q, q)],
                new_momentum[:, pl.ds(start * wide, count * wide)],
                preferred_element_type=jnp.float32,
            )

            @pl.when(half == keeper)
            def _():
                for n in range(count):
                    own[owner, start + n] = sums[:, n * wide:(n + 1) * wide]

            @pl.when(half != keeper)
            def _():
                for n in range(count):
                    send1[owner, start + n] = sums[:, n * wide:(n + 1) * wide].astype(jnp.bfloat16)
                    to_partner(owner, start + n).start()

        def pass_on(owner, j):
            to_partner(owner, j).wait_recv()
            both = own[owner, j] + recv1[owner, j].astype(jnp.float32)
            send2[owner, j] = both.astype(jnp.bfloat16)
            to_rank(owner, me, j).start()

        arrivals = [(peer, c) for c in range(per_rank) for peer in peers]
        coming = [a for a in arrivals if not direct(*a)]

        def forward_next():
            if coming:
                peer, c = coming.pop(0)
                arrived_share(peer, c).wait_recv()
                forward(peer, c, half).start()

        ready, waiting = [], []

        def pieces(new, forward_after, done=()):
            ready.extend(new)
            todo = [
                (owner, j)
                for owner in peers + [me]
                if owner in ready
                for j in (ready if owner in new else new)
                if (owner, j) not in done
            ]
            for n, (owner, j) in enumerate(todo):
                piece(owner, j)
                if n in forward_after:
                    forward_next()
                waiting[:] = [(owner, j, age + 1) for owner, j, age in waiting]
                while waiting and waiting[0][2] >= 2:
                    pass_on(*waiting.pop(0)[:2])
                if owner != me:
                    waiting.append((owner, j, 0))

        mine = [me * per_rank + c for c in range(per_rank)]
        for c in range(per_rank):
            update(mine[c], g_own[:, c * wide:(c + 1) * wide])
        pieces(mine, (1, 3))

        @pl.when(last)
        def _():
            received[...] = jnp.zeros_like(received)

        for peer, c in arrivals:
            j = peer * per_rank + c
            if direct(peer, c):
                before = list(ready)
                for sub in range(subs):
                    for away in range(2):
                        arrived_direct(peer, away, sub).wait_recv()
                    update(j, g_in[peer, c, :, pl.ds(sub * thin, thin)], sub * thin)
                    if subs == 2:
                        for i in before[::per_rank]:
                            half_pieces(j, i, per_rank, sub)
                done = [(j, i) for i in before] if subs == 2 else []
                if done and j != me:

                    @pl.when(half == 0)
                    def _():
                        for item in done:
                            pass_on(*item)

                pieces([j], (0,), done)
                if done and j != me:

                    @pl.when(half == 1)
                    def _():
                        for item in done:
                            pass_on(*item)

                continue
            if (peer, c) in coming:
                forward_next()
            while waiting:
                pass_on(*waiting.pop(0)[:2])
            forward(peer, c, 1 - half).wait_recv()
            update(j, g_in[peer, c])
            pieces([j], (0,))
        while waiting:
            pass_on(*waiting.pop(0)[:2])

        order = ready
        for j in order:
            to_partner(me, j).wait_recv()
            own[me, j] = own[me, j] + recv1[me, j].astype(jnp.float32)
        for j in order[per_rank:] + order[:per_rank]:
            total = own[me, j]
            for peer in peers:
                to_rank(peer, peer, j).wait_recv()
                total = total + recv2[peer, j].astype(jnp.float32)
            gram[:, pl.ds(j * wide, wide)] = total / D

        for peer, c in arrivals:
            if direct(me, c):
                for sub in range(subs):
                    for away in range(2):
                        send_direct(peer, away, sub).wait_send()
            else:
                send_share(peer, c).wait_send()
            if not direct(peer, c):
                forward(peer, c, half).wait_send()
        for j in order:
            for owner in peers + [me]:
                to_partner(owner, j).wait_send()
            for peer in peers:
                to_rank(peer, me, j).wait_send()

    for me in range(ranks):

        @pl.when(rank == me)
        def _():
            as_rank(me)

    @pl.when(jnp.logical_not(first))
    def _():
        shift.wait_send()

    @pl.when(jnp.logical_not(last))
    def _():
        shift.wait_recv()


def write_out(cuts, *refs):
    count = len(cuts)
    sems = refs[-1]
    copies = []
    for i, cut in enumerate(cuts):
        rows = refs[i].shape[-2] // cut
        for n in range(cut):
            place = (slice(None),) * (len(refs[i].shape) - 2) + (pl.ds(n * rows, rows),)
            copies.append(
                pltpu.make_async_copy(
                    refs[i].at[place], refs[count + i].at[place], sems.at[len(copies)]
                )
            )
    for copy in copies:
        copy.start()
    for copy in copies:
        copy.wait()


def on_device(acts, hidden_grad, counts, momentum, act_grad):
    sections, ranks = lax.axis_size("pipe"), lax.axis_size("tensor")
    row_count, features = acts.shape[2:]
    rows, units = momentum.shape[2:]
    width = hidden_grad.shape[3]
    q = PANEL // (2 * ranks)
    wide = 2 * q
    blocks = units // wide
    x_cols = rows if rows % 128 == 0 else features
    bf16, f32 = jnp.bfloat16, jnp.float32
    vmem, dma = pltpu.VMEM, pltpu.SemaphoreType.DMA
    hbm = pl.BlockSpec(memory_space=pltpu.HBM)
    anywhere = pl.BlockSpec(memory_space=pl.ANY)
    in_vmem = pl.BlockSpec(memory_space=vmem)

    def keep(x):
        return pltpu.with_memory_space_constraint(x, pltpu.HBM)

    results = pl.pallas_call(
        functools.partial(kernel, sections, ranks),
        out_shape=(
            vmem((rows, units), bf16),
            vmem((q, units), f32),
            vmem(act_grad.shape, bf16),
        ),
        in_specs=[hbm] * 5,
        out_specs=(in_vmem, in_vmem, in_vmem),
        scratch_shapes=[
            pltpu.SMEM(counts.shape, counts.dtype),
            vmem((row_count, x_cols), bf16),
            vmem((row_count, width), bf16),
            vmem((rows, units), bf16),
            vmem((x_cols, row_count), bf16),
            vmem((ranks, width // wide, row_count, wide), bf16),
            vmem((ranks, wide, rows), bf16),
            vmem((ranks, blocks, q, wide), f32),
            vmem((ranks, blocks, q, wide), bf16),
            vmem((ranks, blocks, q, wide), bf16),
            vmem((ranks, blocks, q, wide), bf16),
            vmem((ranks, blocks, q, wide), bf16),
            dma((4,)), dma, dma,
            dma((ranks, 2, 2)), dma((ranks, 2, 2)),
            dma((ranks, width // wide)), dma((ranks, width // wide)),
            dma((ranks, width // wide)), dma((ranks, width // wide)),
            dma((ranks, blocks)), dma((ranks, blocks)),
            dma((ranks, blocks)), dma((ranks, blocks)),
        ],
        compiler_params=pltpu.CompilerParams(
            collective_id=0, has_side_effects=True, vmem_limit_bytes=32 * 2**20
        ),
    )(keep(acts), keep(hidden_grad), keep(counts), keep(momentum), keep(act_grad))
    new_momentum, gram, received = pl.pallas_call(
        functools.partial(write_out, (4, 2, 2)),
        out_shape=tuple(pltpu.HBM(r.shape, r.dtype) for r in results),
        in_specs=[in_vmem] * 3,
        out_specs=(hbm,) * 3,
        scratch_shapes=[dma((8,))],
    )(*[pltpu.with_memory_space_constraint(r, vmem) for r in results])
    return (new_momentum[None, None], gram[None, None], received)


def solution(mesh):
    return jax.shard_map(
        on_device,
        mesh=mesh,
        in_specs=(
            P("pipe", "expert", None, None),
            P("pipe", None, None, "tensor"),
            P("pipe", None, None),
            P("pipe", "expert", "tensor", None),
            P("pipe", "expert", "tensor"),
        ),
        out_specs=(
            P("pipe", "expert", "tensor", None),
            P("pipe", "expert", "tensor", None),
            P("pipe", "expert", "tensor"),
        ),
        check_vma=False,
    )
```
